256 devices in a mesh: head: 8 (over z_hi, core), tm: 8 (over x, z_lo), height: 4 (over y).
Axes of the slice: x: 4, y: 4, z: 8 (z_hi: 4, z_lo: 2; z = z_hi * 2 + z_lo), core: 2. Of those that a mesh axis runs over, the one named last changes fastest.
Arguments:
- queries: bfloat16 [32, 24, 16, 3072], P('tm', 'height', None, 'head'), may hold values from -6 to 6
- key_tokens: bfloat16 [32, 24, 16, 3072], P('tm', 'height', None, 'head'), may hold values from -6 to 6
- value_tokens: bfloat16 [32, 24, 16, 3072], P('tm', 'height', None, 'head'), may hold values from -6 to 6
- tile_mask: int32 [64, 64], replicated, may hold values from 0 to 1, as said below
Outputs:
- attended: bfloat16 [32, 24, 16, 3072], P('tm', 'height', None, 'head')
The draws below stay inside these ranges and needn't reach their ends.
Inputs may be any that keep to these rules, and one draw needn't show every extreme that they name: tile_mask[a, b] is 1 only where key tile b lies at most one tile row and at most two tile columns away from query tile a, at any distance in frames; tile_mask[a, a] is 1. Other pairs inside that window may be 0.
All inputs are finite; a program needn't handle non-finite values.
Results may differ from the reference program's by a relative error of at most 0.024.
Values may be sent and summed in bfloat16 or wider, within the bound.
A program may use at most 64 MiB of HBM per device.

```python
import math
import jax
import jax.numpy as jnp
from jax import lax

HEADS = 24
HEAD_DIM = 128
COLS = 16
TILE_T = 4
TILE_R = 6
TILE_C = 8
FRAMES = 32
ROWS = 24
CHANNELS = 3072


def normal_part(key, spread_low, spread_high):
    values = jax.random.normal(key, (FRAMES, ROWS, COLS, HEADS * HEAD_DIM), jnp.float32)
    scales = jnp.exp(jax.random.uniform(jax.random.fold_in(key, 1), (FRAMES, ROWS, COLS, 1), jnp.float32, math.log(spread_low), math.log(spread_high)))
    return jnp.clip(values * scales, -6.0, 6.0)


def draw_queries(key, part):
    key = jax.random.fold_in(key, 11)
    drawn = normal_part(key, 1.0, 1.0)
    return drawn.astype(jnp.bfloat16)


def draw_key_tokens(key, part):
    key = jax.random.fold_in(key, 23)
    drawn = normal_part(key, 1.0, 1.0)
    return drawn.astype(jnp.bfloat16)


def draw_tile_mask(key, part):
    key = jax.random.fold_in(key, 37)
    time_tiles = FRAMES // TILE_T
    row_tiles = ROWS // TILE_R
    col_tiles = COLS // TILE_C
    tile_count = time_tiles * row_tiles * col_tiles
    tile_ids = jnp.arange(tile_count, dtype=jnp.int32)
    time_of = tile_ids // (row_tiles * col_tiles)
    row_of = tile_ids // col_tiles % row_tiles
    col_of = tile_ids % col_tiles
    nearby = (jnp.abs(row_of[:, None] - row_of[None, :]) <= 1) & (jnp.abs(col_of[:, None] - col_of[None, :]) <= 2)
    live_frames = jax.random.randint(jax.random.fold_in(key, 1), (), time_tiles // 2 + 1, time_tiles + 1)
    boundary = time_of[None, :] < live_frames
    keeper = jax.random.randint(jax.random.fold_in(key, 2), (tile_count, tile_count), 0, 4) > 0
    itself = tile_ids[:, None] == tile_ids[None, :]
    return (nearby & (boundary & keeper | itself)).astype(jnp.int32)


def steps_of(rng, shape, cuts, low, top_value):
    level, own = 1.0, jax.random.fold_in(rng, 6)
    for axis_at, shards_of in cuts:
        heights = jnp.exp(jax.random.uniform(jax.random.fold_in(own, axis_at), (shards_of,), jnp.float32, low / len(cuts), top_value / len(cuts)))
        level = level * jnp.repeat(heights, shape[axis_at] // shards_of).reshape([-1 if axis == axis_at else 1 for axis in range(len(shape))])
    return level


def gaussian(rng, shape, scale, bound, cuts=(), kind=jnp.bfloat16):
    values = jax.random.normal(rng, shape, jnp.float32) * scale
    if len(cuts) > 0:
        values = steps_of(rng, shape, cuts, -0.22, 0.18) * values
    return jnp.clip(values, min=-bound, max=bound).astype(kind)


def setup_inputs(seed: int = 0) -> dict:
    seeds = jax.random.split(jax.random.key(seed), 5)
    return {
        "queries": draw_queries(jax.random.fold_in(seeds[4], 71), 0),
        "key_tokens": draw_key_tokens(jax.random.fold_in(seeds[4], 71), 0),
        "value_tokens": gaussian(seeds[2], (FRAMES, ROWS, COLS, CHANNELS), 1.0, 6.0, ((0, 8), (1, 4), (3, 8))),
        "tile_mask": draw_tile_mask(jax.random.fold_in(seeds[4], 71), 0),
    }


def reference(queries, key_tokens, value_tokens, tile_mask):
    frame_count, row_count, col_count, chan_count = queries.shape
    head_count = chan_count // HEAD_DIM
    tok_count = frame_count * row_count * col_count
    row_tiles = row_count // TILE_R
    col_tiles = col_count // TILE_C
    frame_part = jnp.arange(frame_count, dtype=jnp.int32) // TILE_T
    row_part = jnp.arange(row_count, dtype=jnp.int32) // TILE_R
    col_part = jnp.arange(col_count, dtype=jnp.int32) // TILE_C
    tile_ids = ((frame_part[:, None, None] * row_tiles + row_part[None, :, None]) * col_tiles + col_part[None, None, :]).reshape(-1)
    query_all = queries.reshape(tok_count, head_count, HEAD_DIM)
    key_all = key_tokens.reshape(tok_count, head_count, HEAD_DIM)
    value_all = value_tokens.reshape(tok_count, head_count, HEAD_DIM)
    per_block = TILE_T * row_count * col_count
    score_scale = HEAD_DIM ** -0.5

    def one_head(head_index):
        query_head = lax.dynamic_index_in_dim(query_all, head_index, 1, keepdims=False)
        key_head = lax.dynamic_index_in_dim(key_all, head_index, 1, keepdims=False)
        value_head = lax.dynamic_index_in_dim(value_all, head_index, 1, keepdims=False)

        def one_block(block_index):
            first_row = (block_index * per_block).astype(jnp.int32)
            query_rows = lax.dynamic_slice_in_dim(query_head, first_row, per_block, 0)
            query_tiles = lax.dynamic_slice_in_dim(tile_ids, first_row, per_block, 0)
            live_mask = tile_mask[query_tiles][:, tile_ids] > 0
            scores = jnp.dot(query_rows, key_head.T, preferred_element_type=jnp.float32) * score_scale
            scores = jnp.where(live_mask, scores, -1e30)
            row_peak = jnp.max(scores, axis=1, keepdims=True)
            raw_weights = jnp.where(live_mask, jnp.exp(scores - row_peak), 0.0)
            weights = raw_weights.astype(jnp.bfloat16)
            result = jnp.dot(weights, value_head, preferred_element_type=jnp.float32) / jnp.sum(raw_weights, axis=1, keepdims=True)
            return result.astype(jnp.bfloat16)

        blocks = lax.map(one_block, jnp.arange(frame_count // TILE_T, dtype=jnp.int32))
        return blocks.reshape(tok_count, HEAD_DIM)

    per_head = lax.map(one_head, jnp.arange(head_count, dtype=jnp.int32))
    return jnp.transpose(per_head, (1, 0, 2)).reshape(frame_count, row_count, col_count, chan_count)
```

```python
import functools

import jax
import jax.numpy as jnp
from jax import lax
from jax.experimental import pallas as pl
from jax.experimental.pallas import tpu as pltpu
from jax.sharding import PartitionSpec as P

HEAD_DIM = 128
TILE_T = 4
TILE_R = 6
TILE_C = 8
MESH = pl.DeviceIdType.MESH
NEG_FILL = -1e30
EXP_SCALE = HEAD_DIM**-0.5 * 1.4426950408889634
NT = (((1,), (1,)), ((), ()))
COL_BLOCKS = (256, 256, 256, 256, 128)
OFFSETS = (0, 3, 1, 2)


def kernel(
    heads, tok,
    q_in, k_in, v_in, mask_ref, out_ref,
    qbuf, kbuf, vbuf, vt, bias, peak, acc, osend, orecv,
    swap_s, swap_r, x_s, x_r, d_s, d_r, q_s, q_r, o_s, o_r,
):
    head = lax.axis_index("head")
    tm = lax.axis_index("tm")
    y = lax.axis_index("height")
    nx = lax.axis_size("tm") // 2
    ny = lax.axis_size("height")
    zh, c = lax.div(head, 2), lax.rem(head, 2)
    x, z = lax.div(tm, 2), lax.rem(tm, 2)
    same = c == z
    inner = jnp.logical_and(y > 0, y < ny - 1)
    own_t = 2 * x + c

    def dev(h, t, r):
        return {"head": h, "tm": t, "height": r}

    partner_head, partner_tm = 2 * zh + z, 2 * x + c
    partner = dev(partner_head, partner_tm, y)
    right = dev(head, 2 * lax.rem(x + 1, nx) + z, y)
    left = dev(head, 2 * lax.rem(x + nx - 1, nx) + z, y)
    sibling = dev(2 * zh + 1 - c, tm, y)

    def remote(src, dst, ssem, rsem, to):
        return pltpu.make_async_remote_copy(
            src_ref=src, dst_ref=dst, send_sem=ssem, recv_sem=rsem, device_id=to, device_id_type=MESH
        )

    barrier = pltpu.get_barrier_semaphore()

    def greet(to):
        pl.semaphore_signal(barrier, inc=1, device_id=to, device_id_type=MESH)

    greet(right)
    greet(left)
    greet(sibling)
    pl.when(y > 0)(lambda: greet(dev(head, tm, y - 1)))
    pl.when(y < ny - 1)(lambda: greet(dev(head, tm, y + 1)))

    @pl.when(jnp.logical_not(same))
    def _():
        greet(partner)
        pl.when(y > 0)(lambda: greet(dev(partner_head, partner_tm, y - 1)))
        pl.when(y < ny - 1)(lambda: greet(dev(partner_head, partner_tm, y + 1)))

    for h in range(heads):
        vt[h] = v_in[:, h * HEAD_DIM : (h + 1) * HEAD_DIM].astype(jnp.float32).T.astype(jnp.bfloat16)
        for t in range(2 * nx):
            vbuf[h, t, HEAD_DIM:] = jnp.ones((16, tok), jnp.bfloat16)
    row_tiles = ny
    tiles = mask_ref.shape[0]
    key_row = lax.broadcasted_iota(jnp.int32, (4 * nx, tiles), 0)
    key_tile = (lax.shift_right_logical(key_row, 1) * row_tiles + y) * 2 + (key_row & 1)
    key_hot = (lax.broadcasted_iota(jnp.int32, (4 * nx, tiles), 1) == key_tile).astype(jnp.bfloat16)
    by_key = lax.dot_general(
        key_hot, mask_ref[...].astype(jnp.float32).astype(jnp.bfloat16), NT, preferred_element_type=jnp.float32
    ).astype(jnp.bfloat16)
    col = lax.broadcasted_iota(jnp.int32, (1, tok), 1)
    col_tile = lax.shift_right_logical(col, 3) & 1
    tile_id = lax.broadcasted_iota(jnp.int32, (tiles, tok), 0)
    q_rows = (y, jnp.where(y > 0, y - 1, y + 1), y + 1)
    for b in range(3):
        q_tile = (own_t * row_tiles + q_rows[b]) * 2 + col_tile
        q_hot = (tile_id == q_tile).astype(jnp.bfloat16)
        live = jnp.dot(by_key, q_hot, preferred_element_type=jnp.float32)
        fill = (1.0 - live) * NEG_FILL
        for i in range(4 * nx):
            bias[i // 4, i // 2 % 2, 8 * (i % 2) : 8 * (i % 2) + 8, b * tok : (b + 1) * tok] = jnp.broadcast_to(
                fill[i : i + 1], (8, tok)
            )

    per_edge = (y > 0).astype(jnp.int32) + (y < ny - 1).astype(jnp.int32)
    pl.semaphore_wait(barrier, 3 + per_edge + jnp.where(same, 0, 1 + per_edge))

    def swap_parts(h):
        cols = slice(h * HEAD_DIM, (h + 1) * HEAD_DIM)
        return (
            (k_in.at[:, cols], lambda t: kbuf.at[h, t]),
            (q_in.at[:, cols], lambda t: qbuf.at[h, pl.ds(0, tok)]),
            (vt.at[h], lambda t: vbuf.at[h, t, pl.ds(0, HEAD_DIM)]),
        )

    for h in range(heads):
        for i, (src, dst) in enumerate(swap_parts(h)):

            @pl.when(same)
            def _(src=src, dst=dst, h=h, i=i):
                pltpu.make_async_copy(src, dst(own_t), swap_r.at[h, i]).start()

            @pl.when(jnp.logical_not(same))
            def _(src=src, dst=dst, h=h, i=i):
                remote(src, dst(2 * x + z), swap_s.at[h, i], swap_r.at[h, i], partner).start()

    def swap_wait(h, i):
        src = (kbuf.at[h, own_t], qbuf.at[h, pl.ds(0, tok)], vbuf.at[h, own_t, pl.ds(0, HEAD_DIM)])[i]

        @pl.when(same)
        def _():
            pltpu.make_async_copy(src, src, swap_r.at[h, i]).wait()

        @pl.when(jnp.logical_not(same))
        def _():
            remote(src, src, swap_s.at[h, i], swap_r.at[h, i], partner).wait_recv()

    def slot(d):
        return 2 * lax.rem(x + OFFSETS[d], nx) + c

    def piece(h, kind, t):
        return kbuf.at[h, t] if kind == 0 else vbuf.at[h, t, pl.ds(0, HEAD_DIM)]

    def x_copy(h, direction, step, kind, d):
        ref = piece(h, kind, slot(d))
        return remote(
            ref, ref, x_s.at[h, direction, step], x_r.at[h, direction, step], right if direction == 0 else left
        )

    def d_copy(h, kind, d, mine=True):
        t = slot(d) if mine else 2 * lax.rem(x + OFFSETS[d], nx) + 1 - c
        ref = piece(h, kind, t)
        return remote(ref, ref, d_s.at[h, d, kind], d_r.at[h, d, kind], sibling)

    def q_copies(h, act):
        src = qbuf.at[h, pl.ds(0, tok)]

        @pl.when(y < ny - 1)
        def _():
            act(remote(src, qbuf.at[h, pl.ds(tok, tok)], q_s.at[h, 0], q_r.at[h, 0], dev(head, tm, y + 1)))

        @pl.when(y > 0)
        def _():
            at = pl.multiple_of(jnp.where(y > 1, 2 * tok, tok), tok)
            act(remote(src, qbuf.at[h, pl.ds(at, tok)], q_s.at[h, 1], q_r.at[h, 1], dev(head, tm, y - 1)))

    def q_wait(h):
        @pl.when(y > 0)
        def _():
            ref = qbuf.at[h, pl.ds(tok, tok)]
            remote(ref, ref, q_s.at[h, 0], q_r.at[h, 0], dev(head, tm, y - 1)).wait_recv()

        @pl.when(y < ny - 1)
        def _():
            at = pl.multiple_of(jnp.where(y > 0, 2 * tok, tok), tok)
            ref = qbuf.at[h, pl.ds(at, tok)]
            remote(ref, ref, q_s.at[h, 1], q_r.at[h, 1], dev(head, tm, y + 1)).wait_recv()

    def send_own(h):
        swap_wait(h, 0)
        x_copy(h, 0, 0, 0, 0).start()
        x_copy(h, 1, 0, 0, 0).start()
        d_copy(h, 0, 0).start()
        swap_wait(h, 1)
        q_copies(h, lambda copy: copy.start())
        swap_wait(h, 2)
        x_copy(h, 0, 1, 1, 0).start()
        x_copy(h, 1, 1, 1, 0).start()
        d_copy(h, 1, 0).start()

    def pass_on(h):
        x_copy(h, 0, 0, 0, 1).wait_recv()
        x_copy(h, 0, 2, 0, 1).start()
        d_copy(h, 0, 1).start()
        x_copy(h, 1, 0, 0, 2).wait_recv()
        d_copy(h, 0, 2).start()
        x_copy(h, 1, 1, 1, 2).wait_recv()
        x_copy(h, 1, 2, 1, 2).start()
        d_copy(h, 1, 2).start()
        x_copy(h, 0, 1, 1, 1).wait_recv()
        d_copy(h, 1, 1).start()

    def take_last(h):
        x_copy(h, 0, 2, 0, 3).wait_recv()
        d_copy(h, 0, 3).start()
        x_copy(h, 1, 2, 1, 3).wait_recv()
        d_copy(h, 1, 3).start()

    edges = [sum(COL_BLOCKS[:i]) for i in range(len(COL_BLOCKS) + 1)]
    blocks = len(COL_BLOCKS)

    def unit(h, d):
        d_copy(h, 0, d, False).wait_recv()
        d_copy(h, 1, d, False).wait_recv()
        first = d == 0
        bx = lax.rem(x + OFFSETS[d], nx)
        state = {}

        def scores(n):
            cols = slice(edges[n], edges[n + 1])
            halves = []
            for p in range(2):
                s = lax.dot_general(
                    kbuf[h, 2 * bx + p], qbuf[h, cols], NT, preferred_element_type=jnp.float32
                )
                halves.append(s.reshape(tok // 16, 16, -1) + bias[bx, p, :, cols][None])
            top = jnp.maximum(jnp.max(halves[0], axis=0), jnp.max(halves[1], axis=0))
            top = jnp.max(top, axis=0, keepdims=True)
            if not first:
                before = peak[:1, cols]
                top = jnp.maximum(before, top)
                state["fade", n] = jnp.exp2((before - top) * EXP_SCALE)
            peak[:1, cols] = top
            state["s", n] = halves
            state["top", n] = top

        def weigh(n):
            top = state["top", n]
            halves = [
                jnp.exp2((s - top[None]) * EXP_SCALE).reshape(tok, -1).astype(jnp.bfloat16)
                for s in state.pop(("s", n))
            ]
            state["w", n] = jnp.concatenate(halves, axis=0)

        def gather(n):
            cols = slice(edges[n], edges[n + 1])
            values = jnp.concatenate([vbuf[h, 2 * bx], vbuf[h, 2 * bx + 1]], axis=1)
            o = jnp.dot(values, state.pop(("w", n)), preferred_element_type=jnp.float32)
            acc[:, cols] = o if first else acc[:, cols] * state["fade", n] + o

        for n in range(blocks + 2):
            if n < blocks:
                scores(n)
            if n >= 2:
                gather(n - 2)
            if 1 <= n <= blocks:
                weigh(n - 1)

    def o_copies(h, act_remote, act_local=None):
        def far(b, row, at):
            return remote(
                osend.at[h, b], orecv.at[h, at], o_s.at[h, b], o_r.at[h, at], dev(partner_head, partner_tm, row)
            )

        if act_local is not None:

            @pl.when(same)
            def _():
                act_local(pltpu.make_async_copy(osend.at[h, 0], orecv.at[h, 1], o_r.at[h, 1]))

        @pl.when(jnp.logical_not(same))
        def _():
            act_remote(far(0, y, 1))

        act_remote(far(1, q_rows[1], jnp.where(y > 0, 2, 0)))
        pl.when(inner)(lambda: act_remote(far(2, y + 1, 0)))

    def finish(h):
        row = lax.broadcasted_iota(jnp.int32, (16, tok), 0)
        for b in range(3):
            cols = slice(b * tok, (b + 1) * tok)
            total = acc[HEAD_DIM : HEAD_DIM + 1, cols]
            osend[h, b, :HEAD_DIM] = (acc[:HEAD_DIM, cols] / total).astype(jnp.bfloat16)
            log = peak[:1, cols] * EXP_SCALE + jnp.log2(total)
            hi = log.astype(jnp.bfloat16).astype(jnp.float32)
            mid = (log - hi).astype(jnp.bfloat16).astype(jnp.float32)
            low = log - hi - mid
            osend[h, b, HEAD_DIM:] = jnp.where(row == 0, hi, jnp.where(row == 1, mid, low)).astype(jnp.bfloat16)
        o_copies(h, lambda copy: copy.start(), lambda copy: copy.start())

    def merge(h):
        def far(at, row):
            ref = orecv.at[h, at]
            remote(ref, ref, o_s.at[h, 0], o_r.at[h, at], dev(partner_head, partner_tm, row)).wait_recv()

        @pl.when(same)
        def _():
            pltpu.make_async_copy(osend.at[h, 0], orecv.at[h, 1], o_r.at[h, 1]).wait()

        pl.when(jnp.logical_not(same))(lambda: far(1, y))
        pl.when(y > 0)(lambda: far(0, y - 1))
        pl.when(y < ny - 1)(lambda: far(2, y + 1))
        there = (y > 0, None, y < ny - 1)
        logs, parts = [], []
        for at in range(3):
            tail = orecv[h, at, HEAD_DIM:].astype(jnp.float32)
            log = tail[0:1] + tail[1:2] + tail[2:3]
            part = orecv[h, at, :HEAD_DIM].astype(jnp.float32)
            if there[at] is not None:
                log = jnp.where(there[at], log, -3e38)
                part = jnp.where(there[at], part, 0.0)
            logs.append(log)
            parts.append(part)
        top = jnp.maximum(jnp.maximum(logs[0], logs[1]), logs[2])
        shares = [jnp.exp2(log - top) for log in logs]
        total = shares[0] + shares[1] + shares[2]
        result = sum(part * (share / total) for part, share in zip(parts, shares))
        out_ref[h] = result.T.astype(jnp.bfloat16)

    send_own(0)
    send_own(1)

    def one_head(h, carry):
        q_wait(h)
        unit(h, 0)
        pass_on(h)
        pl.when(h + 2 < heads)(lambda: send_own(h + 2))
        unit(h, 1)
        unit(h, 2)
        take_last(h)
        pl.when(h > 0)(lambda: merge(h - 1))
        unit(h, 3)
        finish(h)
        return carry

    lax.fori_loop(0, heads, one_head, 0)
    merge(heads - 1)

    def drain(h, carry):
        @pl.when(jnp.logical_not(same))
        def _():
            for i, (src, dst) in enumerate(
                ((kbuf.at[h, 0], 0), (qbuf.at[h, pl.ds(0, tok)], 0), (vt.at[h], 0))
            ):
                remote(src, src, swap_s.at[h, i], swap_r.at[h, i], partner).wait_send()

        for direction in range(2):
            x_copy(h, direction, 0, 0, 0).wait_send()
            x_copy(h, direction, 1, 1, 0).wait_send()
        x_copy(h, 0, 2, 0, 1).wait_send()
        x_copy(h, 1, 2, 1, 2).wait_send()
        for d in range(4):
            d_copy(h, 0, d).wait_send()
            d_copy(h, 1, d).wait_send()
        q_copies(h, lambda copy: copy.wait_send())
        o_copies(h, lambda copy: copy.wait_send())
        return carry

    lax.fori_loop(0, heads, drain, 0)


def solution(mesh):
    times = mesh.shape["tm"]

    def shards(queries, key_tokens, value_tokens, tile_mask):
        frames, rows, cols, chans = queries.shape
        tok = frames * rows * cols
        heads = chans // HEAD_DIM
        bf16, f32 = jnp.bfloat16, jnp.float32
        dma = pltpu.SemaphoreType.DMA
        vmem = pl.BlockSpec(memory_space=pltpu.VMEM)
        out = pl.pallas_call(
            functools.partial(kernel, heads, tok),
            out_shape=jax.ShapeDtypeStruct((heads, tok, HEAD_DIM), bf16),
            in_specs=[vmem] * 4,
            out_specs=vmem,
            scratch_shapes=[
                pltpu.VMEM((heads, 3 * tok, HEAD_DIM), bf16),
                pltpu.VMEM((heads, times, tok, HEAD_DIM), bf16),
                pltpu.VMEM((heads, times, HEAD_DIM + 16, tok), bf16),
                pltpu.VMEM((heads, HEAD_DIM, tok), bf16),
                pltpu.VMEM((times // 2, 2, 16, 3 * tok), f32),
                pltpu.VMEM((8, 3 * tok), f32),
                pltpu.VMEM((HEAD_DIM + 16, 3 * tok), f32),
                pltpu.VMEM((heads, 3, HEAD_DIM + 16, tok), bf16),
                pltpu.VMEM((heads, 3, HEAD_DIM + 16, tok), bf16),
                dma((heads, 3)), dma((heads, 3)),
                dma((heads, 2, 3)), dma((heads, 2, 3)),
                dma((heads, 4, 2)), dma((heads, 4, 2)),
                dma((heads, 2)), dma((heads, 2)),
                dma((heads, 3)), dma((heads, 3)),
            ],
            compiler_params=pltpu.CompilerParams(
                collective_id=0, has_side_effects=True, vmem_limit_bytes=48 * 2**20
            ),
        )(
            queries.reshape(tok, chans),
            key_tokens.reshape(tok, chans),
            value_tokens.reshape(tok, chans),
            tile_mask,
        )
        return jnp.transpose(out, (1, 0, 2)).reshape(frames, rows, cols, chans)

    return jax.shard_map(
        shards,
        mesh=mesh,
        in_specs=(
            P("tm", "height", None, "head"),
            P("tm", "height", None, "head"),
            P("tm", "height", None, "head"),
            P(),
        ),
        out_specs=P("tm", "height", None, "head"),
        check_vma=False,
    )
```

```python
import functools

import jax
import jax.numpy as jnp
from jax import lax
from jax.experimental import pallas as pl
from jax.experimental.pallas import tpu as pltpu
from jax.sharding import PartitionSpec as P

HEAD_DIM = 128
TILE_T = 4
TILE_R = 6
TILE_C = 8
MESH = pl.DeviceIdType.MESH
NEG_FILL = -1e30
EXP_SCALE = HEAD_DIM**-0.5 * 1.4426950408889634
NT = (((1,), (1,)), ((), ()))
FLOOR = -1e29
OFFSETS = (0, 3, 1, 2)
ORDER = (
    (0, 0, 0), (0, 1, 0), (0, 0, 1), (1, 0, 0), (1, 1, 0), (0, 1, 1),
    (1, 0, 1), (2, 0, 0), (2, 1, 0), (1, 1, 1), (2, 0, 1), (2, 1, 1),
)


def kernel(
    heads, tok,
    q_in, k_in, v_in, mask_ref, out_ref,
    qbuf, kbuf, vbuf, v_own, mask, vt, bias, peak, acc, osend, orecv, done, load_s,
    swap_s, swap_r, x_s, x_r, d_s, d_r, q_s, q_r, o_s, o_r, f_s, f_r,
):
    head = lax.axis_index("head")
    tm = lax.axis_index("tm")
    y = lax.axis_index("height")
    nx = lax.axis_size("tm") // 2
    ny = lax.axis_size("height")
    zh, c = lax.div(head, 2), lax.rem(head, 2)
    x, z = lax.div(tm, 2), lax.rem(tm, 2)
    same = c == z
    inner = jnp.logical_and(y > 0, y < ny - 1)
    own_t = 2 * x + c

    def dev(h, t, r):
        return {"head": h, "tm": t, "height": r}

    partner_head, partner_tm = 2 * zh + z, 2 * x + c
    partner = dev(partner_head, partner_tm, y)
    right = dev(head, 2 * lax.rem(x + 1, nx) + z, y)
    left = dev(head, 2 * lax.rem(x + nx - 1, nx) + z, y)
    sibling = dev(2 * zh + 1 - c, tm, y)

    def remote(src, dst, ssem, rsem, to):
        return pltpu.make_async_remote_copy(
            src_ref=src, dst_ref=dst, send_sem=ssem, recv_sem=rsem, device_id=to, device_id_type=MESH
        )

    barrier = pltpu.get_barrier_semaphore()

    def greet(to):
        pl.semaphore_signal(barrier, inc=1, device_id=to, device_id_type=MESH)

    greet(right)
    greet(left)
    greet(sibling)
    pl.when(y > 0)(lambda: greet(dev(head, tm, y - 1)))
    pl.when(y < ny - 1)(lambda: greet(dev(head, tm, y + 1)))

    pl.when(jnp.logical_not(same))(lambda: greet(partner))

    load_v = pltpu.make_async_copy(v_in, v_own, load_s.at[0])
    load_mask = pltpu.make_async_copy(mask_ref, mask, load_s.at[1])
    load_v.start()
    load_mask.start()

    per_edge = (y > 0).astype(jnp.int32) + (y < ny - 1).astype(jnp.int32)
    pl.semaphore_wait(barrier, 3 + per_edge + jnp.where(same, 0, 1))

    def prepare():
        for h in range(heads):
            acc[h] = jnp.zeros(acc.shape[1:], jnp.float32)
            peak[h] = jnp.full(peak.shape[1:], FLOOR, jnp.float32)
            for t in range(2 * nx):
                vbuf[h, t, HEAD_DIM:] = jnp.ones((16, tok), jnp.bfloat16)
        load_mask.wait()
        row_tiles = ny
        tiles = mask.shape[0]
        key_row = lax.broadcasted_iota(jnp.int32, (4 * nx, tiles), 0)
        key_tile = (lax.shift_right_logical(key_row, 1) * row_tiles + y) * 2 + (key_row & 1)
        key_hot = (lax.broadcasted_iota(jnp.int32, (4 * nx, tiles), 1) == key_tile).astype(jnp.bfloat16)
        by_key = lax.dot_general(
            key_hot, mask[...].astype(jnp.float32).astype(jnp.bfloat16), NT, preferred_element_type=jnp.float32
        ).astype(jnp.bfloat16)
        col = lax.broadcasted_iota(jnp.int32, (1, tok), 1)
        col_tile = lax.shift_right_logical(col, 3) & 1
        tile_id = lax.broadcasted_iota(jnp.int32, (tiles, tok), 0)
        for b in range(3):
            q_tile = (own_t * row_tiles + q_rows[b]) * 2 + col_tile
            q_hot = (tile_id == q_tile).astype(jnp.bfloat16)
            live = jnp.dot(by_key, q_hot, preferred_element_type=jnp.float32)
            fill = (1.0 - live) * NEG_FILL
            for i in range(4 * nx):
                bias[i // 2, 8 * (i % 2) : 8 * (i % 2) + 8, b * tok : (b + 1) * tok] = jnp.broadcast_to(
                    fill[i : i + 1], (8, tok)
                )

    q_rows = (y, jnp.where(y > 0, y - 1, y + 1), y + 1)

    def swap_parts(h):
        cols = slice(h * HEAD_DIM, (h + 1) * HEAD_DIM)
        return (
            (q_in.at[:, cols], lambda t: qbuf.at[h, pl.ds(0, tok)]),
            (k_in.at[:, cols], lambda t: kbuf.at[h, t]),
            (vt.at[h], lambda t: vbuf.at[h, t, pl.ds(0, HEAD_DIM)]),
        )

    def swap_start(h, i):
        src, dst = swap_parts(h)[i]

        @pl.when(same)
        def _():
            pltpu.make_async_copy(src, dst(own_t), swap_r.at[h, i]).start()

        @pl.when(jnp.logical_not(same))
        def _():
            remote(src, dst(2 * x + z), swap_s.at[h, i], swap_r.at[h, i], partner).start()

    def swap_wait(h, i):
        src = (qbuf.at[h, pl.ds(0, tok)], kbuf.at[h, own_t], vbuf.at[h, own_t, pl.ds(0, HEAD_DIM)])[i]

        @pl.when(same)
        def _():
            pltpu.make_async_copy(src, src, swap_r.at[h, i]).wait()

        @pl.when(jnp.logical_not(same))
        def _():
            remote(src, src, swap_s.at[h, i], swap_r.at[h, i], partner).wait_recv()

    def block(d):
        return lax.rem(x + OFFSETS[d], nx)

    def slot(d):
        return 2 * block(d) + c

    def piece(h, kind, t):
        return kbuf.at[h, t] if kind == 0 else vbuf.at[h, t, pl.ds(0, HEAD_DIM)]

    def x_copy(h, direction, step, kind, d, src=None):
        ref = piece(h, kind, slot(d))
        return remote(
            ref if src is None else src, ref, x_s.at[h, direction, step], x_r.at[h, direction, step], right if direction == 0 else left
        )

    def d_copy(h, kind, d, mine=True, src=None):
        t = slot(d) if mine else 2 * block(d) + 1 - c
        ref = piece(h, kind, t)
        return remote(ref if src is None else src, ref, d_s.at[h, d, kind], d_r.at[h, d, kind], sibling)

    def q_copies(h, act, src=None):
        src = qbuf.at[h, pl.ds(0, tok)] if src is None else src

        @pl.when(y < ny - 1)
        def _():
            act(remote(src, qbuf.at[h, pl.ds(tok, tok)], q_s.at[h, 0], q_r.at[h, 0], dev(head, tm, y + 1)))

        @pl.when(y > 0)
        def _():
            at = pl.multiple_of(jnp.where(y > 1, 2 * tok, tok), tok)
            act(remote(src, qbuf.at[h, pl.ds(at, tok)], q_s.at[h, 1], q_r.at[h, 1], dev(head, tm, y - 1)))

    def q_wait(h):
        @pl.when(y > 0)
        def _():
            ref = qbuf.at[h, pl.ds(tok, tok)]
            remote(ref, ref, q_s.at[h, 0], q_r.at[h, 0], dev(head, tm, y - 1)).wait_recv()

        @pl.when(y < ny - 1)
        def _():
            at = pl.multiple_of(jnp.where(y > 0, 2 * tok, tok), tok)
            ref = qbuf.at[h, pl.ds(at, tok)]
            remote(ref, ref, q_s.at[h, 1], q_r.at[h, 1], dev(head, tm, y + 1)).wait_recv()

    def send_part(h, i, src=None):
        if i == 0:
            q_copies(h, lambda copy: copy.start(), src)
        else:
            kind = i - 1
            x_copy(h, 0, kind, kind, 0, src).start()
            x_copy(h, 1, kind, kind, 0, src).start()
            d_copy(h, kind, 0, True, src).start()

    def begin(h, i):
        if (h, i) == (0, 2):
            load_v.wait()
        if i == 2:
            vt[h] = v_own[:, h * HEAD_DIM : (h + 1) * HEAD_DIM].astype(jnp.float32).T.astype(jnp.bfloat16)
        swap_start(h, i)
        if h < 2:
            pl.when(same)(lambda: send_part(h, i, swap_parts(h)[i][0]))

    def own_part(h, i):
        swap_wait(h, i)
        if h < 2:
            pl.when(jnp.logical_not(same))(lambda: send_part(h, i))
        else:
            send_part(h, i)

    def pass_on(h):
        x_copy(h, 0, 0, 0, 1).wait_recv()
        x_copy(h, 0, 2, 0, 1).start()
        d_copy(h, 0, 1).start()
        x_copy(h, 1, 0, 0, 2).wait_recv()
        d_copy(h, 0, 2).start()
        x_copy(h, 1, 1, 1, 2).wait_recv()
        x_copy(h, 1, 2, 1, 2).start()
        d_copy(h, 1, 2).start()
        x_copy(h, 0, 1, 1, 1).wait_recv()
        d_copy(h, 1, 1).start()

    def take_last(h):
        x_copy(h, 0, 2, 0, 3).wait_recv()
        d_copy(h, 0, 3).start()
        x_copy(h, 1, 2, 1, 3).wait_recv()
        d_copy(h, 1, 3).start()

    def unit(h, pair, e):
        @pl.when(jnp.logical_not(same) if e == 0 else same)
        def _():
            for i in range(2):
                d_copy(h, 0, 2 * pair + i, False).wait_recv()
                d_copy(h, 1, 2 * pair + i, False).wait_recv()

        parity = z if e == 0 else 1 - z
        times = [2 * block(2 * pair + i) + parity for i in range(2)]
        state = {}

        def scores(n):
            cols = slice(n * tok, (n + 1) * tok)
            halves, tops = [], []
            for t in times:
                s = lax.dot_general(kbuf[h, t], qbuf[h, cols], NT, preferred_element_type=jnp.float32)
                s = s.reshape(tok // 16, 16, tok)
                halves.append(s)
                tops.append(jnp.max(s, axis=0) + bias[t, :, cols])
            top = jnp.max(jnp.maximum(tops[0], tops[1]), axis=0, keepdims=True)
            before = peak[h, :1, cols]
            top = jnp.maximum(before, top)
            state["fade", n] = jnp.exp2((before - top) * EXP_SCALE)
            peak[h, :1, cols] = top
            state["s", n] = halves
            state["top", n] = top

        def weigh(n):
            cols = slice(n * tok, (n + 1) * tok)
            parts = []
            for t, s in zip(times, state.pop(("s", n))):
                shift = (bias[t, :, cols] - state["top", n]) * EXP_SCALE
                parts.append(jnp.exp2(s * EXP_SCALE + shift[None]).reshape(tok, tok).astype(jnp.bfloat16))
            state["w", n] = jnp.concatenate(parts, axis=0)

        def gather(n):
            cols = slice(n * tok, (n + 1) * tok)
            values = jnp.concatenate([vbuf[h, t] for t in times], axis=1)
            o = jnp.dot(values, state.pop(("w", n)), preferred_element_type=jnp.float32)
            acc[h, :, cols] = acc[h, :, cols] * state["fade", n] + o

        for n in range(5):
            if n < 3:
                scores(n)
            if n >= 2:
                gather(n - 2)
            if 1 <= n <= 3:
                weigh(n - 1)

    def o_copies(h, act):
        def far(b, row, at):
            return remote(osend.at[h, b], orecv.at[h, at], o_s.at[h, b], o_r.at[h, at], dev(head, tm, row))

        act(far(0, q_rows[1], jnp.where(y > 0, 1, 0)))
        pl.when(inner)(lambda: act(far(1, y + 1, 0)))

    def log_of(h, cols):
        total = jnp.maximum(acc[h, HEAD_DIM : HEAD_DIM + 1, cols], 1e-30)
        return total, peak[h, :1, cols] * EXP_SCALE + jnp.log2(total)

    def finish(h):
        row = lax.broadcasted_iota(jnp.int32, (16, tok), 0)
        for b in (1, 2):
            cols = slice(b * tok, (b + 1) * tok)
            total, log = log_of(h, cols)
            osend[h, b - 1, :HEAD_DIM] = (acc[h, :HEAD_DIM, cols] * (1.0 / total)).astype(jnp.bfloat16)
            hi = log.astype(jnp.bfloat16).astype(jnp.float32)
            mid = (log - hi).astype(jnp.bfloat16).astype(jnp.float32)
            low = log - hi - mid
            osend[h, b - 1, HEAD_DIM:] = jnp.where(row == 0, hi, jnp.where(row == 1, mid, low)).astype(jnp.bfloat16)
        o_copies(h, lambda copy: copy.start())

    def out_cols(h):
        return out_ref.at[:, h * HEAD_DIM : (h + 1) * HEAD_DIM]

    def merge(h):
        def far(at, row):
            ref = orecv.at[h, at]
            remote(ref, ref, o_s.at[h, 0], o_r.at[h, at], dev(head, tm, row)).wait_recv()

        pl.when(y > 0)(lambda: far(0, y - 1))
        pl.when(y < ny - 1)(lambda: far(1, y + 1))
        there = (y > 0, y < ny - 1)
        total, log = log_of(h, slice(0, tok))
        logs, parts = [log], [acc[h, :HEAD_DIM, :tok]]
        for at in range(2):
            tail = orecv[h, at, HEAD_DIM:].astype(jnp.float32)
            logs.append(jnp.where(there[at], tail[0:1] + tail[1:2] + tail[2:3], -3e38))
            parts.append(jnp.where(there[at], orecv[h, at, :HEAD_DIM].astype(jnp.float32), 0.0))
        top = jnp.maximum(jnp.maximum(logs[0], logs[1]), logs[2])
        shares = [jnp.exp2(log - top) for log in logs]
        scale = 1.0 / (shares[0] + shares[1] + shares[2])
        shares[0] = shares[0] / total
        result = sum(part * (share * scale) for part, share in zip(parts, shares))
        done[h] = result.T.astype(jnp.bfloat16)

        @pl.when(same)
        def _():
            pltpu.make_async_copy(done.at[h], out_cols(h), f_r.at[h]).start()

        @pl.when(jnp.logical_not(same))
        def _():
            remote(done.at[h], out_cols(h), f_s.at[h], f_r.at[h], partner).start()

    for h in range(heads):
        for i in range(3):
            begin(h, i)
    prepare()
    for i in range(3):
        own_part(0, i)

    events_same = {
        0: [(q_wait, 0), (pass_on, 0), (own_part, 2, 0), (own_part, 2, 1), (own_part, 2, 2)],
        1: [(pass_on, 1), (take_last, 0)],
        2: [(own_part, 1, 0), (own_part, 1, 1), (own_part, 1, 2)],
        3: [(q_wait, 1), (pass_on, 2)],
        4: [(take_last, 1)],
        7: [(q_wait, 2), (take_last, 2)],
    }
    events_swapped = {
        0: [(q_wait, 0), (own_part, 1, 0)],
        1: [(own_part, 1, 1), (own_part, 1, 2)],
        2: [(pass_on, 0)],
        3: [(own_part, 2, 0), (q_wait, 1)],
        4: [(own_part, 2, 1), (pass_on, 1)],
        5: [(own_part, 2, 2), (take_last, 0)],
        7: [(q_wait, 2), (pass_on, 2)],
        8: [(take_last, 1)],
        11: [(take_last, 2)],
    }
    last_of = {h: max(i for i, (g, _, _) in enumerate(ORDER) if g == h) for h in range(heads)}

    for n, (h, pair, e) in enumerate(ORDER):
        for table, role in ((events_same, same), (events_swapped, jnp.logical_not(same))):

            @pl.when(role)
            def _(acts=table.get(n, ())):
                for act, *which in acts:
                    act(*which)

        unit(h, pair, e)
        if n == last_of[h]:
            finish(h)
        for g in range(heads - 1):
            if n == last_of[g] + 2:
                merge(g)

    merge(heads - 1)
    for h in range(heads):

        @pl.when(same)
        def _(h=h):
            pltpu.make_async_copy(done.at[h], out_cols(h), f_r.at[h]).wait()

        @pl.when(jnp.logical_not(same))
        def _(h=h):
            copy = remote(done.at[h], out_cols(h), f_s.at[h], f_r.at[h], partner)
            copy.wait_send()
            copy.wait_recv()

    def drain(h, carry):
        @pl.when(jnp.logical_not(same))
        def _():
            for i, (src, dst) in enumerate(
                ((qbuf.at[h, pl.ds(0, tok)], 0), (kbuf.at[h, 0], 0), (vt.at[h], 0))
            ):
                remote(src, src, swap_s.at[h, i], swap_r.at[h, i], partner).wait_send()

        for direction in range(2):
            x_copy(h, direction, 0, 0, 0).wait_send()
            x_copy(h, direction, 1, 1, 0).wait_send()
        x_copy(h, 0, 2, 0, 1).wait_send()
        x_copy(h, 1, 2, 1, 2).wait_send()
        for d in range(4):
            d_copy(h, 0, d).wait_send()
            d_copy(h, 1, d).wait_send()
        q_copies(h, lambda copy: copy.wait_send())
        o_copies(h, lambda copy: copy.wait_send())
        return carry

    lax.fori_loop(0, heads, drain, 0)


def solution(mesh):
    times = mesh.shape["tm"]

    def shards(queries, key_tokens, value_tokens, tile_mask):
        frames, rows, cols, chans = queries.shape
        tok = frames * rows * cols
        heads = chans // HEAD_DIM
        bf16, f32 = jnp.bfloat16, jnp.float32
        dma = pltpu.SemaphoreType.DMA
        out = pl.pallas_call(
            functools.partial(kernel, heads, tok),
            out_shape=jax.ShapeDtypeStruct((tok, chans), bf16),
            in_specs=[pl.BlockSpec(memory_space=pl.ANY)] * 4,
            out_specs=pl.BlockSpec(memory_space=pl.ANY),
            scratch_shapes=[
                pltpu.VMEM((heads, 3 * tok, HEAD_DIM), bf16),
                pltpu.VMEM((heads, times, tok, HEAD_DIM), bf16),
                pltpu.VMEM((heads, times, HEAD_DIM + 16, tok), bf16),
                pltpu.VMEM((tok, chans), bf16),
                pltpu.VMEM(tile_mask.shape, jnp.int32),
                pltpu.VMEM((heads, HEAD_DIM, tok), bf16),
                pltpu.VMEM((times, 16, 3 * tok), f32),
                pltpu.VMEM((heads, 8, 3 * tok), f32),
                pltpu.VMEM((heads, HEAD_DIM + 16, 3 * tok), f32),
                pltpu.VMEM((heads, 2, HEAD_DIM + 16, tok), bf16),
                pltpu.VMEM((heads, 2, HEAD_DIM + 16, tok), bf16),
                pltpu.VMEM((heads, tok, HEAD_DIM), bf16),
                dma((2,)),
                dma((heads, 3)), dma((heads, 3)),
                dma((heads, 2, 3)), dma((heads, 2, 3)),
                dma((heads, 4, 2)), dma((heads, 4, 2)),
                dma((heads, 2)), dma((heads, 2)),
                dma((heads, 2)), dma((heads, 2)),
                dma((heads,)), dma((heads,)),
            ],
            compiler_params=pltpu.CompilerParams(
                collective_id=0, has_side_effects=True, vmem_limit_bytes=60 * 2**20
            ),
        )(
            queries.reshape(tok, chans),
            key_tokens.reshape(tok, chans),
            value_tokens.reshape(tok, chans),
            tile_mask,
        )
        return out.reshape(frames, rows, cols, chans)

    return jax.shard_map(
        shards,
        mesh=mesh,
        in_specs=(
            P("tm", "height", None, "head"),
            P("tm", "height", None, "head"),
            P("tm", "height", None, "head"),
            P(),
        ),
        out_specs=P("tm", "height", None, "head"),
        check_vma=False,
    )
```

```python
import functools

import jax
import jax.numpy as jnp
from jax import lax
from jax.experimental import pallas as pl
from jax.experimental.pallas import tpu as pltpu
from jax.sharding import PartitionSpec as P

HEAD_DIM = 128
TILE_T = 4
TILE_R = 6
TILE_C = 8
MESH = pl.DeviceIdType.MESH
NEG_FILL = -1e30
EXP_SCALE = HEAD_DIM**-0.5 * 1.4426950408889634
NT = (((1,), (1,)), ((), ()))
FLOOR = -1e29
OFFSETS = (0, 3, 1, 2)
OWN, NEAR = ((0, 256), (256, 384)), ((384, 640), (640, 896), (896, 1152))


def kernel(
    heads, tok,
    q_in, k_in, v_in, mask_ref, out_ref,
    qbuf, kbuf, vbuf, v_own, mask, vt, bias, peak, acc, osend, orecv, done, load_s,
    swap_s, swap_r, x_s, x_r, d_s, d_r, q_s, q_r, o_s, o_r, f_s, f_r,
):
    head = lax.axis_index("head")
    tm = lax.axis_index("tm")
    y = lax.axis_index("height")
    nx = lax.axis_size("tm") // 2
    ny = lax.axis_size("height")
    zh, c = lax.div(head, 2), lax.rem(head, 2)
    x, z = lax.div(tm, 2), lax.rem(tm, 2)
    same = c == z
    inner = jnp.logical_and(y > 0, y < ny - 1)
    own_t = 2 * x + c

    def dev(h, t, r):
        return {"head": h, "tm": t, "height": r}

    partner_head, partner_tm = 2 * zh + z, 2 * x + c
    partner = dev(partner_head, partner_tm, y)
    right = dev(head, 2 * lax.rem(x + 1, nx) + z, y)
    left = dev(head, 2 * lax.rem(x + nx - 1, nx) + z, y)
    sibling = dev(2 * zh + 1 - c, tm, y)

    def remote(src, dst, ssem, rsem, to):
        return pltpu.make_async_remote_copy(
            src_ref=src, dst_ref=dst, send_sem=ssem, recv_sem=rsem, device_id=to, device_id_type=MESH
        )

    barrier = pltpu.get_barrier_semaphore()

    def greet(to):
        pl.semaphore_signal(barrier, inc=1, device_id=to, device_id_type=MESH)

    greet(right)
    greet(left)
    greet(sibling)
    pl.when(y > 0)(lambda: greet(dev(head, tm, y - 1)))
    pl.when(y < ny - 1)(lambda: greet(dev(head, tm, y + 1)))

    pl.when(jnp.logical_not(same))(lambda: greet(partner))

    load_v = pltpu.make_async_copy(v_in, v_own, load_s.at[0])
    load_mask = pltpu.make_async_copy(mask_ref, mask, load_s.at[1])
    load_v.start()
    load_mask.start()

    per_edge = (y > 0).astype(jnp.int32) + (y < ny - 1).astype(jnp.int32)
    pl.semaphore_wait(barrier, 3 + per_edge + jnp.where(same, 0, 1))

    def prepare():
        for h in range(heads):
            acc[h] = jnp.zeros(acc.shape[1:], jnp.float32)
            peak[h] = jnp.full(peak.shape[1:], FLOOR, jnp.float32)
            for t in range(2 * nx):
                vbuf[h, t, HEAD_DIM:] = jnp.ones((16, tok), jnp.bfloat16)
        load_mask.wait()
        row_tiles = ny
        tiles = mask.shape[0]
        key_row = lax.broadcasted_iota(jnp.int32, (4 * nx, tiles), 0)
        key_tile = (lax.shift_right_logical(key_row, 1) * row_tiles + y) * 2 + (key_row & 1)
        key_hot = (lax.broadcasted_iota(jnp.int32, (4 * nx, tiles), 1) == key_tile).astype(jnp.bfloat16)
        by_key = lax.dot_general(
            key_hot, mask[...].astype(jnp.float32).astype(jnp.bfloat16), NT, preferred_element_type=jnp.float32
        ).astype(jnp.bfloat16)
        col = lax.broadcasted_iota(jnp.int32, (1, tok), 1)
        col_tile = lax.shift_right_logical(col, 3) & 1
        tile_id = lax.broadcasted_iota(jnp.int32, (tiles, tok), 0)
        for b in range(3):
            q_tile = (own_t * row_tiles + q_rows[b]) * 2 + col_tile
            q_hot = (tile_id == q_tile).astype(jnp.bfloat16)
            live = jnp.dot(by_key, q_hot, preferred_element_type=jnp.float32)
            fill = (1.0 - live) * NEG_FILL
            for i in range(4 * nx):
                bias[i // 2, 8 * (i % 2) : 8 * (i % 2) + 8, b * tok : (b + 1) * tok] = jnp.broadcast_to(
                    fill[i : i + 1], (8, tok)
                )

    q_rows = (y, jnp.where(y > 0, y - 1, y + 1), y + 1)

    def swap_parts(h):
        cols = slice(h * HEAD_DIM, (h + 1) * HEAD_DIM)
        return (
            (q_in.at[:, cols], lambda t: qbuf.at[h, pl.ds(0, tok)]),
            (k_in.at[:, cols], lambda t: kbuf.at[h, t]),
            (vt.at[h], lambda t: vbuf.at[h, t, pl.ds(0, HEAD_DIM)]),
        )

    def swap_start(h, i):
        src, dst = swap_parts(h)[i]

        @pl.when(same)
        def _():
            pltpu.make_async_copy(src, dst(own_t), swap_r.at[h, i]).start()

        @pl.when(jnp.logical_not(same))
        def _():
            remote(src, dst(2 * x + z), swap_s.at[h, i], swap_r.at[h, i], partner).start()

    def swap_wait(h, i):
        src = (qbuf.at[h, pl.ds(0, tok)], kbuf.at[h, own_t], vbuf.at[h, own_t, pl.ds(0, HEAD_DIM)])[i]

        @pl.when(same)
        def _():
            pltpu.make_async_copy(src, src, swap_r.at[h, i]).wait()

        @pl.when(jnp.logical_not(same))
        def _():
            remote(src, src, swap_s.at[h, i], swap_r.at[h, i], partner).wait_recv()

    def block(d):
        return lax.rem(x + OFFSETS[d], nx)

    def slot(d):
        return 2 * block(d) + c

    def piece(h, kind, t):
        return kbuf.at[h, t] if kind == 0 else vbuf.at[h, t, pl.ds(0, HEAD_DIM)]

    def x_copy(h, direction, step, kind, d, src=None):
        ref = piece(h, kind, slot(d))
        return remote(
            ref if src is None else src, ref, x_s.at[h, direction, step], x_r.at[h, direction, step], right if direction == 0 else left
        )

    def d_copy(h, kind, d, mine=True, src=None):
        t = slot(d) if mine else 2 * block(d) + 1 - c
        ref = piece(h, kind, t)
        return remote(ref if src is None else src, ref, d_s.at[h, d, kind], d_r.at[h, d, kind], sibling)

    def q_copies(h, act, src=None):
        src = qbuf.at[h, pl.ds(0, tok)] if src is None else src

        @pl.when(y < ny - 1)
        def _():
            act(remote(src, qbuf.at[h, pl.ds(tok, tok)], q_s.at[h, 0], q_r.at[h, 0], dev(head, tm, y + 1)))

        @pl.when(y > 0)
        def _():
            at = pl.multiple_of(jnp.where(y > 1, 2 * tok, tok), tok)
            act(remote(src, qbuf.at[h, pl.ds(at, tok)], q_s.at[h, 1], q_r.at[h, 1], dev(head, tm, y - 1)))

    def q_wait(h):
        @pl.when(y > 0)
        def _():
            ref = qbuf.at[h, pl.ds(tok, tok)]
            remote(ref, ref, q_s.at[h, 0], q_r.at[h, 0], dev(head, tm, y - 1)).wait_recv()

        @pl.when(y < ny - 1)
        def _():
            at = pl.multiple_of(jnp.where(y > 0, 2 * tok, tok), tok)
            ref = qbuf.at[h, pl.ds(at, tok)]
            remote(ref, ref, q_s.at[h, 1], q_r.at[h, 1], dev(head, tm, y + 1)).wait_recv()

    def send_part(h, i, src=None):
        if i == 0:
            q_copies(h, lambda copy: copy.start(), src)
        else:
            kind = i - 1
            x_copy(h, 0, kind, kind, 0, src).start()
            x_copy(h, 1, kind, kind, 0, src).start()
            d_copy(h, kind, 0, True, src).start()

    def begin(h, i):
        if (h, i) == (0, 2):
            load_v.wait()
        if i == 2:
            vt[h] = v_own[:, h * HEAD_DIM : (h + 1) * HEAD_DIM].astype(jnp.float32).T.astype(jnp.bfloat16)
        swap_start(h, i)
        if h < 2:
            pl.when(same)(lambda: send_part(h, i, swap_parts(h)[i][0]))

    def own_part(h, i):
        swap_wait(h, i)
        if h < 2:
            pl.when(jnp.logical_not(same))(lambda: send_part(h, i))
        else:
            send_part(h, i)

    def pass_on(h):
        x_copy(h, 0, 0, 0, 1).wait_recv()
        x_copy(h, 0, 2, 0, 1).start()
        d_copy(h, 0, 1).start()
        x_copy(h, 1, 0, 0, 2).wait_recv()
        d_copy(h, 0, 2).start()
        x_copy(h, 1, 1, 1, 2).wait_recv()
        x_copy(h, 1, 2, 1, 2).start()
        d_copy(h, 1, 2).start()
        x_copy(h, 0, 1, 1, 1).wait_recv()
        d_copy(h, 1, 1).start()

    def take_last(h):
        x_copy(h, 0, 2, 0, 3).wait_recv()
        d_copy(h, 0, 3).start()
        x_copy(h, 1, 2, 1, 3).wait_recv()
        d_copy(h, 1, 3).start()

    def work(units):
        for e in range(2):
            pieces = [(h, 2 * pair + i) for _, h, pair, g in units if g == e for i in range(2)]
            pieces = [piece for piece in pieces if (piece, e) not in taken]
            taken.update((piece, e) for piece in pieces)

            @pl.when(jnp.logical_not(same) if e == 0 else same)
            def _(pieces=pieces):
                for h, d in pieces:
                    d_copy(h, 0, d, False).wait_recv()
                    d_copy(h, 1, d, False).wait_recv()

        tasks = [(h, pair, e, slice(*cols)) for columns, h, pair, e in units for cols in columns]
        state = {}

        def times(pair, e):
            return [2 * block(2 * pair + i) + (z if e == 0 else 1 - z) for i in range(2)]

        def scores(n):
            h, pair, e, cols = tasks[n]
            parts, tops = [], []
            for t in times(pair, e):
                s = lax.dot_general(kbuf[h, t], qbuf[h, cols], NT, preferred_element_type=jnp.float32)
                s = s.reshape(tok // 16, 16, -1)
                parts.append(s)
                tops.append(jnp.max(s, axis=0) + bias[t, :, cols])
            top = jnp.max(jnp.maximum(tops[0], tops[1]), axis=0, keepdims=True)
            before = peak[h, :1, cols]
            top = jnp.maximum(before, top)
            peak[h, :1, cols] = top
            state[n] = parts, top, jnp.exp2((before - top) * EXP_SCALE)

        def weigh(n):
            h, pair, e, cols = tasks[n]
            parts, top, fade = state[n]
            weights = []
            for t, s in zip(times(pair, e), parts):
                shift = (bias[t, :, cols] - top) * EXP_SCALE
                weights.append(jnp.exp2(s * EXP_SCALE + shift[None]).reshape(tok, -1).astype(jnp.bfloat16))
            state[n] = jnp.concatenate(weights, axis=0), fade

        def gather(n):
            h, pair, e, cols = tasks[n]
            weights, fade = state.pop(n)
            values = jnp.concatenate([vbuf[h, t] for t in times(pair, e)], axis=1)
            acc[h, :, cols] = acc[h, :, cols] * fade + jnp.dot(values, weights, preferred_element_type=jnp.float32)

        for n in range(len(tasks) + 2):
            if n < len(tasks):
                scores(n)
            if n >= 2:
                gather(n - 2)
            if 1 <= n <= len(tasks):
                weigh(n - 1)

    def o_copies(h, act):
        def far(b, row, at):
            return remote(osend.at[h, b], orecv.at[h, at], o_s.at[h, b], o_r.at[h, at], dev(head, tm, row))

        act(far(0, q_rows[1], jnp.where(y > 0, 1, 0)))
        pl.when(inner)(lambda: act(far(1, y + 1, 0)))

    def log_of(h, cols):
        total = jnp.maximum(acc[h, HEAD_DIM : HEAD_DIM + 1, cols], 1e-30)
        return total, peak[h, :1, cols] * EXP_SCALE + jnp.log2(total)

    def finish(h):
        row = lax.broadcasted_iota(jnp.int32, (16, tok), 0)
        for b in (1, 2):
            cols = slice(b * tok, (b + 1) * tok)
            total, log = log_of(h, cols)
            osend[h, b - 1, :HEAD_DIM] = (acc[h, :HEAD_DIM, cols] * (1.0 / total)).astype(jnp.bfloat16)
            hi = log.astype(jnp.bfloat16).astype(jnp.float32)
            mid = (log - hi).astype(jnp.bfloat16).astype(jnp.float32)
            low = log - hi - mid
            osend[h, b - 1, HEAD_DIM:] = jnp.where(row == 0, hi, jnp.where(row == 1, mid, low)).astype(jnp.bfloat16)
        o_copies(h, lambda copy: copy.start())

    def out_cols(h):
        return out_ref.at[:, h * HEAD_DIM : (h + 1) * HEAD_DIM]

    def merge(h):
        def far(at, row):
            ref = orecv.at[h, at]
            remote(ref, ref, o_s.at[h, 0], o_r.at[h, at], dev(head, tm, row)).wait_recv()

        pl.when(y > 0)(lambda: far(0, y - 1))
        pl.when(y < ny - 1)(lambda: far(1, y + 1))
        there = (y > 0, y < ny - 1)
        total, log = log_of(h, slice(0, tok))
        logs, parts = [log], [acc[h, :HEAD_DIM, :tok]]
        for at in range(2):
            tail = orecv[h, at, HEAD_DIM:].astype(jnp.float32)
            logs.append(jnp.where(there[at], tail[0:1] + tail[1:2] + tail[2:3], -3e38))
            parts.append(jnp.where(there[at], orecv[h, at, :HEAD_DIM].astype(jnp.float32), 0.0))
        top = jnp.maximum(jnp.maximum(logs[0], logs[1]), logs[2])
        shares = [jnp.exp2(log - top) for log in logs]
        scale = 1.0 / (shares[0] + shares[1] + shares[2])
        shares[0] = shares[0] / total
        result = sum(part * (share * scale) for part, share in zip(parts, shares))
        done[h] = result.T.astype(jnp.bfloat16)

        @pl.when(same)
        def _():
            pltpu.make_async_copy(done.at[h], out_cols(h), f_r.at[h]).start()

        @pl.when(jnp.logical_not(same))
        def _():
            remote(done.at[h], out_cols(h), f_s.at[h], f_r.at[h], partner).start()

    for h, i in [(h, i) for h in range(2) for i in range(3)] + [(2, 1), (2, 2), (2, 0)]:
        begin(h, i)
    prepare()
    for i in range(3):
        own_part(0, i)

    taken = set()
    steps = [
        ([(pass_on, 0)], [], [(OWN, 0, 0, 0)], []),
        (
            [(own_part, 2, 0), (own_part, 2, 1), (own_part, 2, 2), (pass_on, 1)]
            + [(own_part, 1, i) for i in range(3)]
            + [(q_wait, 0)],
            [(own_part, 1, 0), (own_part, 1, 1), (q_wait, 0)],
            [(NEAR, 0, 0, 0), (OWN, 1, 0, 0)],
            [],
        ),
        ([(take_last, 0)], [(own_part, 1, 2), (own_part, 2, 1)], [(NEAR, 0, 1, 0)], []),
        (
            [(q_wait, 1)],
            [(pass_on, 0), (own_part, 2, 2), (own_part, 2, 0), (q_wait, 1)],
            [(NEAR, 0, 0, 1), (NEAR, 1, 0, 0)],
            [],
        ),
        ([(pass_on, 2), (take_last, 1)], [], [(OWN, 0, 1, 0), (OWN, 0, 0, 1)], []),
        ([(q_wait, 2)], [(pass_on, 1), (q_wait, 2)], [(NEAR, 2, 0, 0), (NEAR, 1, 0, 1)], []),
        ([(take_last, 2)], [(take_last, 0)], [(NEAR, 1, 1, 0), (NEAR, 0, 1, 1)], [(finish, 0)]),
        ([], [(pass_on, 2), (take_last, 1)], [(NEAR, 1, 1, 1), (NEAR, 2, 1, 0)], [(finish, 1)]),
        ([], [], [(OWN, 0, 1, 1), (OWN, 1, 1, 0), (NEAR, 2, 0, 1)], []),
        ([], [(take_last, 2)], [(NEAR, 2, 1, 1)], [(finish, 2)]),
        ([], [], [(OWN, 1, 0, 1), (OWN, 1, 1, 1)], [(merge, 0)]),
        ([], [], [(OWN, 2, 0, 0), (OWN, 2, 1, 0), (OWN, 2, 0, 1), (OWN, 2, 1, 1)], [(merge, 1), (merge, 2)]),
    ]

    def do(acts):
        for act, *which in acts:
            act(*which)

    for acts_same, acts_swapped, units, acts_then in steps:
        pl.when(same)(lambda: do(acts_same))
        pl.when(jnp.logical_not(same))(lambda: do(acts_swapped))
        work(units)
        do(acts_then)

    for h in range(heads):

        @pl.when(same)
        def _(h=h):
            pltpu.make_async_copy(done.at[h], out_cols(h), f_r.at[h]).wait()

        @pl.when(jnp.logical_not(same))
        def _(h=h):
            copy = remote(done.at[h], out_cols(h), f_s.at[h], f_r.at[h], partner)
            copy.wait_send()
            copy.wait_recv()

    def drain(h, carry):
        @pl.when(jnp.logical_not(same))
        def _():
            for i, (src, dst) in enumerate(
                ((qbuf.at[h, pl.ds(0, tok)], 0), (kbuf.at[h, 0], 0), (vt.at[h], 0))
            ):
                remote(src, src, swap_s.at[h, i], swap_r.at[h, i], partner).wait_send()

        for direction in range(2):
            x_copy(h, direction, 0, 0, 0).wait_send()
            x_copy(h, direction, 1, 1, 0).wait_send()
        x_copy(h, 0, 2, 0, 1).wait_send()
        x_copy(h, 1, 2, 1, 2).wait_send()
        for d in range(4):
            d_copy(h, 0, d).wait_send()
            d_copy(h, 1, d).wait_send()
        q_copies(h, lambda copy: copy.wait_send())
        o_copies(h, lambda copy: copy.wait_send())
        return carry

    lax.fori_loop(0, heads, drain, 0)


def solution(mesh):
    times = mesh.shape["tm"]

    def shards(queries, key_tokens, value_tokens, tile_mask):
        frames, rows, cols, chans = queries.shape
        tok = frames * rows * cols
        heads = chans // HEAD_DIM
        bf16, f32 = jnp.bfloat16, jnp.float32
        dma = pltpu.SemaphoreType.DMA
        out = pl.pallas_call(
            functools.partial(kernel, heads, tok),
            out_shape=jax.ShapeDtypeStruct((tok, chans), bf16),
            in_specs=[pl.BlockSpec(memory_space=pl.ANY)] * 4,
            out_specs=pl.BlockSpec(memory_space=pl.ANY),
            scratch_shapes=[
                pltpu.VMEM((heads, 3 * tok, HEAD_DIM), bf16),
                pltpu.VMEM((heads, times, tok, HEAD_DIM), bf16),
                pltpu.VMEM((heads, times, HEAD_DIM + 16, tok), bf16),
                pltpu.VMEM((tok, chans), bf16),
                pltpu.VMEM(tile_mask.shape, jnp.int32),
                pltpu.VMEM((heads, HEAD_DIM, tok), bf16),
                pltpu.VMEM((times, 16, 3 * tok), f32),
                pltpu.VMEM((heads, 8, 3 * tok), f32),
                pltpu.VMEM((heads, HEAD_DIM + 16, 3 * tok), f32),
                pltpu.VMEM((heads, 2, HEAD_DIM + 16, tok), bf16),
                pltpu.VMEM((heads, 2, HEAD_DIM + 16, tok), bf16),
                pltpu.VMEM((heads, tok, HEAD_DIM), bf16),
                dma((2,)),
                dma((heads, 3)), dma((heads, 3)),
                dma((heads, 2, 3)), dma((heads, 2, 3)),
                dma((heads, 4, 2)), dma((heads, 4, 2)),
                dma((heads, 2)), dma((heads, 2)),
                dma((heads, 2)), dma((heads, 2)),
                dma((heads,)), dma((heads,)),
            ],
            compiler_params=pltpu.CompilerParams(
                collective_id=0, has_side_effects=True, vmem_limit_bytes=60 * 2**20
            ),
        )(
            queries.reshape(tok, chans),
            key_tokens.reshape(tok, chans),
            value_tokens.reshape(tok, chans),
            tile_mask,
        )
        return out.reshape(frames, rows, cols, chans)

    return jax.shard_map(
        shards,
        mesh=mesh,
        in_specs=(
            P("tm", "height", None, "head"),
            P("tm", "height", None, "head"),
            P("tm", "height", None, "head"),
            P(),
        ),
        out_specs=P("tm", "height", None, "head"),
        check_vma=False,
    )
```

```python
import functools

import jax
import jax.numpy as jnp
from jax import lax
from jax.experimental import pallas as pl
from jax.experimental.pallas import tpu as pltpu
from jax.sharding import PartitionSpec as P

HEAD_DIM = 128
TILE_T = 4
TILE_R = 6
TILE_C = 8
MESH = pl.DeviceIdType.MESH
NEG_FILL = -1e30
EXP_SCALE = HEAD_DIM**-0.5 * 1.4426950408889634
NT = (((1,), (1,)), ((), ()))
FLOOR = -1e29
OFFSETS = (0, 3, 1, 2)
OWN, NEAR = ((0, 256), (256, 384)), ((384, 640), (640, 896), (896, 1152))


def kernel(
    heads, tok,
    q_in, k_in, v_in, mask_ref, out_ref,
    qbuf, kbuf, vbuf, v_own, mask, vt, bias, peak, acc, osend, orecv, done, load_s,
    swap_s, swap_r, x_s, x_r, d_s, d_r, q_s, q_r, o_s, o_r, f_s, f_r,
):
    head = lax.axis_index("head")
    tm = lax.axis_index("tm")
    y = lax.axis_index("height")
    nx = lax.axis_size("tm") // 2
    ny = lax.axis_size("height")
    zh, c = lax.div(head, 2), lax.rem(head, 2)
    x, z = lax.div(tm, 2), lax.rem(tm, 2)
    same = c == z
    inner = jnp.logical_and(y > 0, y < ny - 1)
    own_t = 2 * x + c

    def dev(h, t, r):
        return {"head": h, "tm": t, "height": r}

    partner_head, partner_tm = 2 * zh + z, 2 * x + c
    partner = dev(partner_head, partner_tm, y)
    right = dev(head, 2 * lax.rem(x + 1, nx) + z, y)
    left = dev(head, 2 * lax.rem(x + nx - 1, nx) + z, y)
    sibling = dev(2 * zh + 1 - c, tm, y)

    def remote(src, dst, ssem, rsem, to):
        return pltpu.make_async_remote_copy(
            src_ref=src, dst_ref=dst, send_sem=ssem, recv_sem=rsem, device_id=to, device_id_type=MESH
        )

    barrier = pltpu.get_barrier_semaphore()

    def greet(to):
        pl.semaphore_signal(barrier, inc=1, device_id=to, device_id_type=MESH)

    greet(right)
    greet(left)
    greet(sibling)
    pl.when(y > 0)(lambda: greet(dev(head, tm, y - 1)))
    pl.when(y < ny - 1)(lambda: greet(dev(head, tm, y + 1)))

    pl.when(jnp.logical_not(same))(lambda: greet(partner))

    load_v = pltpu.make_async_copy(v_in, v_own, load_s.at[0])
    load_mask = pltpu.make_async_copy(mask_ref, mask, load_s.at[1])
    load_v.start()
    load_mask.start()

    per_edge = (y > 0).astype(jnp.int32) + (y < ny - 1).astype(jnp.int32)
    pl.semaphore_wait(barrier, 3 + per_edge + jnp.where(same, 0, 1))

    def prepare():
        for h in range(heads):
            acc[h] = jnp.zeros(acc.shape[1:], jnp.float32)
            peak[h] = jnp.full(peak.shape[1:], FLOOR, jnp.float32)
            for t in range(2 * nx):
                vbuf[h, t, HEAD_DIM:] = jnp.ones((16, tok), jnp.bfloat16)
        load_mask.wait()
        row_tiles = ny
        tiles = mask.shape[0]
        key_row = lax.broadcasted_iota(jnp.int32, (4 * nx, tiles), 0)
        key_tile = (lax.shift_right_logical(key_row, 1) * row_tiles + y) * 2 + (key_row & 1)
        key_hot = (lax.broadcasted_iota(jnp.int32, (4 * nx, tiles), 1) == key_tile).astype(jnp.bfloat16)
        by_key = lax.dot_general(
            key_hot, mask[...].astype(jnp.float32).astype(jnp.bfloat16), NT, preferred_element_type=jnp.float32
        ).astype(jnp.bfloat16)
        col = lax.broadcasted_iota(jnp.int32, (1, tok), 1)
        col_tile = lax.shift_right_logical(col, 3) & 1
        tile_id = lax.broadcasted_iota(jnp.int32, (tiles, tok), 0)
        for b in range(3):
            q_tile = (own_t * row_tiles + q_rows[b]) * 2 + col_tile
            q_hot = (tile_id == q_tile).astype(jnp.bfloat16)
            live = jnp.dot(by_key, q_hot, preferred_element_type=jnp.float32)
            fill = (1.0 - live) * NEG_FILL
            for i in range(4 * nx):
                bias[i // 2, 8 * (i % 2) : 8 * (i % 2) + 8, b * tok : (b + 1) * tok] = jnp.broadcast_to(
                    fill[i : i + 1], (8, tok)
                )

    q_rows = (y, jnp.where(y > 0, y - 1, y + 1), y + 1)

    def swap_parts(h):
        cols = slice(h * HEAD_DIM, (h + 1) * HEAD_DIM)
        return (
            (q_in.at[:, cols], lambda t: qbuf.at[h, pl.ds(0, tok)]),
            (k_in.at[:, cols], lambda t: kbuf.at[h, t]),
            (vt.at[h], lambda t: vbuf.at[h, t, pl.ds(0, HEAD_DIM)]),
        )

    def swap_start(h, i):
        src, dst = swap_parts(h)[i]

        @pl.when(same)
        def _():
            pltpu.make_async_copy(src, dst(own_t), swap_r.at[h, i]).start()

        @pl.when(jnp.logical_not(same))
        def _():
            remote(src, dst(2 * x + z), swap_s.at[h, i], swap_r.at[h, i], partner).start()

    def swap_wait(h, i):
        src = (qbuf.at[h, pl.ds(0, tok)], kbuf.at[h, own_t], vbuf.at[h, own_t, pl.ds(0, HEAD_DIM)])[i]

        @pl.when(same)
        def _():
            pltpu.make_async_copy(src, src, swap_r.at[h, i]).wait()

        @pl.when(jnp.logical_not(same))
        def _():
            remote(src, src, swap_s.at[h, i], swap_r.at[h, i], partner).wait_recv()

    def block(d):
        return lax.rem(x + OFFSETS[d], nx)

    def slot(d):
        return 2 * block(d) + c

    def piece(h, kind, t):
        return kbuf.at[h, t] if kind == 0 else vbuf.at[h, t, pl.ds(0, HEAD_DIM)]

    def x_copy(h, direction, step, kind, d, src=None):
        ref = piece(h, kind, slot(d))
        return remote(
            ref if src is None else src, ref, x_s.at[h, direction, step], x_r.at[h, direction, step], right if direction == 0 else left
        )

    def d_copy(h, kind, d, mine=True, src=None):
        t = slot(d) if mine else 2 * block(d) + 1 - c
        ref = piece(h, kind, t)
        return remote(ref if src is None else src, ref, d_s.at[h, d, kind], d_r.at[h, d, kind], sibling)

    def q_copies(h, act, src=None):
        src = qbuf.at[h, pl.ds(0, tok)] if src is None else src

        @pl.when(y < ny - 1)
        def _():
            act(remote(src, qbuf.at[h, pl.ds(tok, tok)], q_s.at[h, 0], q_r.at[h, 0], dev(head, tm, y + 1)))

        @pl.when(y > 0)
        def _():
            at = pl.multiple_of(jnp.where(y > 1, 2 * tok, tok), tok)
            act(remote(src, qbuf.at[h, pl.ds(at, tok)], q_s.at[h, 1], q_r.at[h, 1], dev(head, tm, y - 1)))

    def q_wait(h):
        @pl.when(y > 0)
        def _():
            ref = qbuf.at[h, pl.ds(tok, tok)]
            remote(ref, ref, q_s.at[h, 0], q_r.at[h, 0], dev(head, tm, y - 1)).wait_recv()

        @pl.when(y < ny - 1)
        def _():
            at = pl.multiple_of(jnp.where(y > 0, 2 * tok, tok), tok)
            ref = qbuf.at[h, pl.ds(at, tok)]
            remote(ref, ref, q_s.at[h, 1], q_r.at[h, 1], dev(head, tm, y + 1)).wait_recv()

    def send_part(h, i, src=None):
        if i == 0:
            q_copies(h, lambda copy: copy.start(), src)
        else:
            kind = i - 1
            d_copy(h, kind, 0, True, src).start()
            x_copy(h, 0, kind, kind, 0, src).start()
            x_copy(h, 1, kind, kind, 0, src).start()

    def begin(h, i):
        if (h, i) == (0, 2):
            load_v.wait()
        if i == 2:
            vt[h] = v_own[:, h * HEAD_DIM : (h + 1) * HEAD_DIM].astype(jnp.float32).T.astype(jnp.bfloat16)
        swap_start(h, i)
        if h < 2:
            pl.when(same)(lambda: send_part(h, i, swap_parts(h)[i][0]))

    def own_part(h, i):
        swap_wait(h, i)
        if h < 2:
            pl.when(jnp.logical_not(same))(lambda: send_part(h, i))
        else:
            send_part(h, i)

    def pass_on(h):
        x_copy(h, 0, 0, 0, 1).wait_recv()
        d_copy(h, 0, 1).start()
        x_copy(h, 0, 2, 0, 1).start()
        x_copy(h, 1, 0, 0, 2).wait_recv()
        d_copy(h, 0, 2).start()
        x_copy(h, 1, 1, 1, 2).wait_recv()
        d_copy(h, 1, 2).start()
        x_copy(h, 1, 2, 1, 2).start()
        x_copy(h, 0, 1, 1, 1).wait_recv()
        d_copy(h, 1, 1).start()

    def take_last(h):
        x_copy(h, 0, 2, 0, 3).wait_recv()
        d_copy(h, 0, 3).start()
        x_copy(h, 1, 2, 1, 3).wait_recv()
        d_copy(h, 1, 3).start()

    def work(units):
        for e in range(2):
            pieces = [(h, 2 * pair + i) for _, h, pair, g in units if g == e for i in range(2)]
            pieces = [piece for piece in pieces if (piece, e) not in taken]
            taken.update((piece, e) for piece in pieces)

            @pl.when(jnp.logical_not(same) if e == 0 else same)
            def _(pieces=pieces):
                for h, d in pieces:
                    d_copy(h, 0, d, False).wait_recv()
                    d_copy(h, 1, d, False).wait_recv()

        tasks = [(h, pair, e, slice(*cols)) for columns, h, pair, e in units for cols in columns]
        state = {}

        def times(pair, e):
            return [2 * block(2 * pair + i) + (z if e == 0 else 1 - z) for i in range(2)]

        def scores(n):
            h, pair, e, cols = tasks[n]
            parts, tops = [], []
            for t in times(pair, e):
                s = lax.dot_general(kbuf[h, t], qbuf[h, cols], NT, preferred_element_type=jnp.float32)
                s = s.reshape(tok // 16, 16, -1)
                parts.append(s)
                tops.append(jnp.max(s, axis=0) + bias[t, :, cols])
            top = jnp.max(jnp.maximum(tops[0], tops[1]), axis=0, keepdims=True)
            before = peak[h, :1, cols]
            top = jnp.maximum(before, top)
            peak[h, :1, cols] = top
            state[n] = parts, top, jnp.exp2((before - top) * EXP_SCALE)

        def weigh(n):
            h, pair, e, cols = tasks[n]
            parts, top, fade = state[n]
            weights = []
            for t, s in zip(times(pair, e), parts):
                shift = (bias[t, :, cols] - top) * EXP_SCALE
                weights.append(jnp.exp2(s * EXP_SCALE + shift[None]).reshape(tok, -1).astype(jnp.bfloat16))
            state[n] = jnp.concatenate(weights, axis=0), fade

        def gather(n):
            h, pair, e, cols = tasks[n]
            weights, fade = state.pop(n)
            values = jnp.concatenate([vbuf[h, t] for t in times(pair, e)], axis=1)
            acc[h, :, cols] = acc[h, :, cols] * fade + jnp.dot(values, weights, preferred_element_type=jnp.float32)

        for n in range(len(tasks) + 2):
            if n < len(tasks):
                scores(n)
            if n >= 2:
                gather(n - 2)
            if 1 <= n <= len(tasks):
                weigh(n - 1)

    def o_copies(h, act):
        def far(b, row, at):
            return remote(osend.at[h, b], orecv.at[h, at], o_s.at[h, b], o_r.at[h, at], dev(head, tm, row))

        act(far(0, q_rows[1], jnp.where(y > 0, 1, 0)))
        pl.when(inner)(lambda: act(far(1, y + 1, 0)))

    def log_of(h, cols):
        total = jnp.maximum(acc[h, HEAD_DIM : HEAD_DIM + 1, cols], 1e-30)
        return total, peak[h, :1, cols] * EXP_SCALE + jnp.log2(total)

    def finish(h):
        row = lax.broadcasted_iota(jnp.int32, (16, tok), 0)
        for b in (1, 2):
            cols = slice(b * tok, (b + 1) * tok)
            total, log = log_of(h, cols)
            osend[h, b - 1, :HEAD_DIM] = (acc[h, :HEAD_DIM, cols] * (1.0 / total)).astype(jnp.bfloat16)
            hi = log.astype(jnp.bfloat16).astype(jnp.float32)
            mid = (log - hi).astype(jnp.bfloat16).astype(jnp.float32)
            low = log - hi - mid
            osend[h, b - 1, HEAD_DIM:] = jnp.where(row == 0, hi, jnp.where(row == 1, mid, low)).astype(jnp.bfloat16)
        pl.when(jnp.logical_not(same))(lambda: o_copies(h, lambda copy: copy.start()))

    def finish_same(h):
        pl.when(same)(lambda: o_copies(h, lambda copy: copy.start()))

    def out_cols(h):
        return out_ref.at[:, h * HEAD_DIM : (h + 1) * HEAD_DIM]

    def merge(h):
        def far(at, row):
            ref = orecv.at[h, at]
            remote(ref, ref, o_s.at[h, 0], o_r.at[h, at], dev(head, tm, row)).wait_recv()

        pl.when(y > 0)(lambda: far(0, y - 1))
        pl.when(y < ny - 1)(lambda: far(1, y + 1))
        there = (y > 0, y < ny - 1)
        total, log = log_of(h, slice(0, tok))
        logs, parts = [log], [acc[h, :HEAD_DIM, :tok]]
        for at in range(2):
            tail = orecv[h, at, HEAD_DIM:].astype(jnp.float32)
            logs.append(jnp.where(there[at], tail[0:1] + tail[1:2] + tail[2:3], -3e38))
            parts.append(jnp.where(there[at], orecv[h, at, :HEAD_DIM].astype(jnp.float32), 0.0))
        top = jnp.maximum(jnp.maximum(logs[0], logs[1]), logs[2])
        shares = [jnp.exp2(log - top) for log in logs]
        scale = 1.0 / (shares[0] + shares[1] + shares[2])
        shares[0] = shares[0] / total
        result = sum(part * (share * scale) for part, share in zip(parts, shares))
        done[h] = result.T.astype(jnp.bfloat16)

        @pl.when(same)
        def _():
            pltpu.make_async_copy(done.at[h], out_cols(h), f_r.at[h]).start()

        @pl.when(jnp.logical_not(same))
        def _():
            remote(done.at[h], out_cols(h), f_s.at[h], f_r.at[h], partner).start()

    for h, i in [(h, i) for h in range(2) for i in range(3)] + [(2, 1), (2, 2), (2, 0)]:
        begin(h, i)
    prepare()
    for i in range(3):
        own_part(0, i)

    taken = set()
    steps = [
        ([(pass_on, 0)], [], [(OWN, 0, 0, 0)], []),
        (
            [(own_part, 2, 0), (own_part, 2, 1), (own_part, 2, 2), (pass_on, 1)]
            + [(own_part, 1, i) for i in range(3)]
            + [(q_wait, 0)],
            [(own_part, 1, 0), (own_part, 1, 1), (q_wait, 0)],
            [(NEAR, 0, 0, 0), (OWN, 1, 0, 0)],
            [],
        ),
        ([(take_last, 0)], [(own_part, 1, 2), (own_part, 2, 1)], [(NEAR, 0, 1, 0)], []),
        (
            [(q_wait, 1)],
            [(pass_on, 0), (own_part, 2, 2), (own_part, 2, 0), (q_wait, 1)],
            [(NEAR, 0, 0, 1), (NEAR, 1, 0, 0)],
            [],
        ),
        ([(pass_on, 2), (take_last, 1)], [], [(OWN, 0, 1, 0), (OWN, 0, 0, 1)], []),
        ([(q_wait, 2)], [(pass_on, 1), (q_wait, 2)], [(NEAR, 2, 0, 0), (NEAR, 1, 0, 1)], []),
        ([(take_last, 2)], [(take_last, 0)], [(NEAR, 1, 1, 0), (NEAR, 0, 1, 1)], [(finish, 0), (finish_same, 0)]),
        ([], [(pass_on, 2), (take_last, 1)], [(NEAR, 1, 1, 1), (NEAR, 2, 1, 0)], [(finish, 1), (finish_same, 1)]),
        ([], [], [(OWN, 0, 1, 1), (OWN, 1, 1, 0), (NEAR, 2, 0, 1)], []),
        ([], [(take_last, 2)], [(NEAR, 2, 1, 1)], [(finish, 2)]),
        ([], [], [(OWN, 1, 0, 1), (OWN, 1, 1, 1)], [(finish_same, 2), (merge, 0)]),
        ([], [], [(OWN, 2, 0, 0), (OWN, 2, 1, 0)], [(merge, 1)]),
        ([], [], [(OWN, 2, 0, 1), (OWN, 2, 1, 1)], [(merge, 2)]),
    ]

    def do(acts):
        for act, *which in acts:
            act(*which)

    for acts_same, acts_swapped, units, acts_then in steps:
        pl.when(same)(lambda: do(acts_same))
        pl.when(jnp.logical_not(same))(lambda: do(acts_swapped))
        work(units)
        do(acts_then)

    for h in range(heads):

        @pl.when(same)
        def _(h=h):
            pltpu.make_async_copy(done.at[h], out_cols(h), f_r.at[h]).wait()

        @pl.when(jnp.logical_not(same))
        def _(h=h):
            copy = remote(done.at[h], out_cols(h), f_s.at[h], f_r.at[h], partner)
            copy.wait_send()
            copy.wait_recv()

    def drain(h, carry):
        @pl.when(jnp.logical_not(same))
        def _():
            for i, (src, dst) in enumerate(
                ((qbuf.at[h, pl.ds(0, tok)], 0), (kbuf.at[h, 0], 0), (vt.at[h], 0))
            ):
                remote(src, src, swap_s.at[h, i], swap_r.at[h, i], partner).wait_send()

        for direction in range(2):
            x_copy(h, direction, 0, 0, 0).wait_send()
            x_copy(h, direction, 1, 1, 0).wait_send()
        x_copy(h, 0, 2, 0, 1).wait_send()
        x_copy(h, 1, 2, 1, 2).wait_send()
        for d in range(4):
            d_copy(h, 0, d).wait_send()
            d_copy(h, 1, d).wait_send()
        q_copies(h, lambda copy: copy.wait_send())
        o_copies(h, lambda copy: copy.wait_send())
        return carry

    lax.fori_loop(0, heads, drain, 0)


def solution(mesh):
    times = mesh.shape["tm"]

    def shards(queries, key_tokens, value_tokens, tile_mask):
        frames, rows, cols, chans = queries.shape
        tok = frames * rows * cols
        heads = chans // HEAD_DIM
        bf16, f32 = jnp.bfloat16, jnp.float32
        dma = pltpu.SemaphoreType.DMA
        out = pl.pallas_call(
            functools.partial(kernel, heads, tok),
            out_shape=jax.ShapeDtypeStruct((tok, chans), bf16),
            in_specs=[pl.BlockSpec(memory_space=pl.ANY)] * 4,
            out_specs=pl.BlockSpec(memory_space=pl.ANY),
            scratch_shapes=[
                pltpu.VMEM((heads, 3 * tok, HEAD_DIM), bf16),
                pltpu.VMEM((heads, times, tok, HEAD_DIM), bf16),
                pltpu.VMEM((heads, times, HEAD_DIM + 16, tok), bf16),
                pltpu.VMEM((tok, chans), bf16),
                pltpu.VMEM(tile_mask.shape, jnp.int32),
                pltpu.VMEM((heads, HEAD_DIM, tok), bf16),
                pltpu.VMEM((times, 16, 3 * tok), f32),
                pltpu.VMEM((heads, 8, 3 * tok), f32),
                pltpu.VMEM((heads, HEAD_DIM + 16, 3 * tok), f32),
                pltpu.VMEM((heads, 2, HEAD_DIM + 16, tok), bf16),
                pltpu.VMEM((heads, 2, HEAD_DIM + 16, tok), bf16),
                pltpu.VMEM((heads, tok, HEAD_DIM), bf16),
                dma((2,)),
                dma((heads, 3)), dma((heads, 3)),
                dma((heads, 2, 3)), dma((heads, 2, 3)),
                dma((heads, 4, 2)), dma((heads, 4, 2)),
                dma((heads, 2)), dma((heads, 2)),
                dma((heads, 2)), dma((heads, 2)),
                dma((heads,)), dma((heads,)),
            ],
            compiler_params=pltpu.CompilerParams(
                collective_id=0, has_side_effects=True, vmem_limit_bytes=536 * 2**20 // 10
            ),
        )(
            queries.reshape(tok, chans),
            key_tokens.reshape(tok, chans),
            value_tokens.reshape(tok, chans),
            tile_mask,
        )
        return out.reshape(frames, rows, cols, chans)

    return jax.shard_map(
        shards,
        mesh=mesh,
        in_specs=(
            P("tm", "height", None, "head"),
            P("tm", "height", None, "head"),
            P("tm", "height", None, "head"),
            P(),
        ),
        out_specs=P("tm", "height", None, "head"),
        check_vma=False,
    )
```

```python
import functools

import jax
import jax.numpy as jnp
from jax import lax
from jax.experimental import pallas as pl
from jax.experimental.pallas import tpu as pltpu
from jax.sharding import PartitionSpec as P

HEAD_DIM = 128
TILE_T = 4
TILE_R = 6
TILE_C = 8
MESH = pl.DeviceIdType.MESH
NEG_FILL = -1e30
EXP_SCALE = HEAD_DIM**-0.5 * 1.4426950408889634
NT = (((1,), (1,)), ((), ()))
FLOOR = -1e29
OFFSETS = (0, 3, 1, 2)
CHUNKS = ((0, 256), (256, 384))
OWN, NEAR = ((0, 256), (256, 384)), ((384, 640), (640, 896), (896, 1152))


def kernel(
    heads, tok,
    q_in, k_in, v_in, mask_ref, out_ref,
    qbuf, kbuf, vbuf, v_own, mask, vt, bias, peak, acc, osend, orecv, done, load_s,
    swap_s, swap_r, x_s, x_r, d_s, d_r, q_s, q_r, o_s, o_r, f_s, f_r,
):
    head = lax.axis_index("head")
    tm = lax.axis_index("tm")
    y = lax.axis_index("height")
    nx = lax.axis_size("tm") // 2
    ny = lax.axis_size("height")
    zh, c = lax.div(head, 2), lax.rem(head, 2)
    x, z = lax.div(tm, 2), lax.rem(tm, 2)
    same = c == z
    inner = jnp.logical_and(y > 0, y < ny - 1)
    own_t = 2 * x + c

    def dev(h, t, r):
        return {"head": h, "tm": t, "height": r}

    partner_head, partner_tm = 2 * zh + z, 2 * x + c
    partner = dev(partner_head, partner_tm, y)
    right = dev(head, 2 * lax.rem(x + 1, nx) + z, y)
    left = dev(head, 2 * lax.rem(x + nx - 1, nx) + z, y)
    sibling = dev(2 * zh + 1 - c, tm, y)

    def remote(src, dst, ssem, rsem, to):
        return pltpu.make_async_remote_copy(
            src_ref=src, dst_ref=dst, send_sem=ssem, recv_sem=rsem, device_id=to, device_id_type=MESH
        )

    barrier = pltpu.get_barrier_semaphore()

    def greet(to):
        pl.semaphore_signal(barrier, inc=1, device_id=to, device_id_type=MESH)

    greet(right)
    greet(left)
    greet(sibling)
    pl.when(y > 0)(lambda: greet(dev(head, tm, y - 1)))
    pl.when(y < ny - 1)(lambda: greet(dev(head, tm, y + 1)))

    pl.when(jnp.logical_not(same))(lambda: greet(partner))

    load_v = pltpu.make_async_copy(v_in, v_own, load_s.at[0])
    load_mask = pltpu.make_async_copy(mask_ref, mask, load_s.at[1])
    load_v.start()
    load_mask.start()

    per_edge = (y > 0).astype(jnp.int32) + (y < ny - 1).astype(jnp.int32)
    pl.semaphore_wait(barrier, 3 + per_edge + jnp.where(same, 0, 1))

    def prepare():
        for h in range(heads):
            acc[h] = jnp.zeros(acc.shape[1:], jnp.float32)
            peak[h] = jnp.full(peak.shape[1:], FLOOR, jnp.float32)
            for t in range(2 * nx):
                vbuf[h, t, HEAD_DIM:] = jnp.ones((16, tok), jnp.bfloat16)
        load_mask.wait()
        row_tiles = ny
        tiles = mask.shape[0]
        key_row = lax.broadcasted_iota(jnp.int32, (4 * nx, tiles), 0)
        key_tile = (lax.shift_right_logical(key_row, 1) * row_tiles + y) * 2 + (key_row & 1)
        key_hot = (lax.broadcasted_iota(jnp.int32, (4 * nx, tiles), 1) == key_tile).astype(jnp.bfloat16)
        by_key = lax.dot_general(
            key_hot, mask[...].astype(jnp.float32).astype(jnp.bfloat16), NT, preferred_element_type=jnp.float32
        ).astype(jnp.bfloat16)
        col = lax.broadcasted_iota(jnp.int32, (1, tok), 1)
        col_tile = lax.shift_right_logical(col, 3) & 1
        tile_id = lax.broadcasted_iota(jnp.int32, (tiles, tok), 0)
        for b in range(3):
            q_tile = (own_t * row_tiles + q_rows[b]) * 2 + col_tile
            q_hot = (tile_id == q_tile).astype(jnp.bfloat16)
            live = jnp.dot(by_key, q_hot, preferred_element_type=jnp.float32)
            fill = (1.0 - live) * NEG_FILL
            for i in range(4 * nx):
                bias[i // 2, 8 * (i % 2) : 8 * (i % 2) + 8, b * tok : (b + 1) * tok] = jnp.broadcast_to(
                    fill[i : i + 1], (8, tok)
                )

    q_rows = (y, jnp.where(y > 0, y - 1, y + 1), y + 1)

    def swap_parts(h):
        cols = slice(h * HEAD_DIM, (h + 1) * HEAD_DIM)
        return (
            (q_in.at[:, cols], lambda t: qbuf.at[h, pl.ds(0, tok)]),
            (k_in.at[:, cols], lambda t: kbuf.at[h, t]),
            (vt.at[h], lambda t: vbuf.at[h, t, pl.ds(0, HEAD_DIM)]),
        )

    def swap_start(h, i):
        src, dst = swap_parts(h)[i]

        @pl.when(same)
        def _():
            pltpu.make_async_copy(src, dst(own_t), swap_r.at[h, i]).start()

        @pl.when(jnp.logical_not(same))
        def _():
            remote(src, dst(2 * x + z), swap_s.at[h, i], swap_r.at[h, i], partner).start()

    def swap_wait(h, i):
        src = (qbuf.at[h, pl.ds(0, tok)], kbuf.at[h, own_t], vbuf.at[h, own_t, pl.ds(0, HEAD_DIM)])[i]

        @pl.when(same)
        def _():
            pltpu.make_async_copy(src, src, swap_r.at[h, i]).wait()

        @pl.when(jnp.logical_not(same))
        def _():
            remote(src, src, swap_s.at[h, i], swap_r.at[h, i], partner).wait_recv()

    def block(d):
        return lax.rem(x + OFFSETS[d], nx)

    def slot(d):
        return 2 * block(d) + c

    def piece(h, kind, t):
        return kbuf.at[h, t] if kind == 0 else vbuf.at[h, t, pl.ds(0, HEAD_DIM)]

    def x_copy(h, direction, step, kind, d, src=None):
        ref = piece(h, kind, slot(d))
        return remote(
            ref if src is None else src, ref, x_s.at[h, direction, step], x_r.at[h, direction, step], right if direction == 0 else left
        )

    def d_copy(h, kind, d, mine=True, src=None):
        t = slot(d) if mine else 2 * block(d) + 1 - c
        ref = piece(h, kind, t)
        return remote(ref if src is None else src, ref, d_s.at[h, d, kind], d_r.at[h, d, kind], sibling)

    def q_copies(h, act, src=None):
        src = qbuf.at[h, pl.ds(0, tok)] if src is None else src

        @pl.when(y < ny - 1)
        def _():
            act(remote(src, qbuf.at[h, pl.ds(tok, tok)], q_s.at[h, 0], q_r.at[h, 0], dev(head, tm, y + 1)))

        @pl.when(y > 0)
        def _():
            at = pl.multiple_of(jnp.where(y > 1, 2 * tok, tok), tok)
            act(remote(src, qbuf.at[h, pl.ds(at, tok)], q_s.at[h, 1], q_r.at[h, 1], dev(head, tm, y - 1)))

    def q_wait(h):
        @pl.when(y > 0)
        def _():
            ref = qbuf.at[h, pl.ds(tok, tok)]
            remote(ref, ref, q_s.at[h, 0], q_r.at[h, 0], dev(head, tm, y - 1)).wait_recv()

        @pl.when(y < ny - 1)
        def _():
            at = pl.multiple_of(jnp.where(y > 0, 2 * tok, tok), tok)
            ref = qbuf.at[h, pl.ds(at, tok)]
            remote(ref, ref, q_s.at[h, 1], q_r.at[h, 1], dev(head, tm, y + 1)).wait_recv()

    def send_part(h, i, src=None):
        if i == 0:
            q_copies(h, lambda copy: copy.start(), src)
        else:
            kind = i - 1
            d_copy(h, kind, 0, True, src).start()
            x_copy(h, 0, kind, kind, 0, src).start()
            x_copy(h, 1, kind, kind, 0, src).start()

    def begin(h, i):
        if (h, i) == (0, 2):
            load_v.wait()
        if i == 2:
            vt[h] = v_own[:, h * HEAD_DIM : (h + 1) * HEAD_DIM].astype(jnp.float32).T.astype(jnp.bfloat16)
        swap_start(h, i)
        if h < 2:
            pl.when(same)(lambda: send_part(h, i, swap_parts(h)[i][0]))

    def own_part(h, i):
        swap_wait(h, i)
        if h < 2:
            pl.when(jnp.logical_not(same))(lambda: send_part(h, i))
        else:
            send_part(h, i)

    def pass_on(h):
        x_copy(h, 0, 0, 0, 1).wait_recv()
        d_copy(h, 0, 1).start()
        x_copy(h, 0, 2, 0, 1).start()
        x_copy(h, 1, 0, 0, 2).wait_recv()
        d_copy(h, 0, 2).start()
        x_copy(h, 1, 1, 1, 2).wait_recv()
        d_copy(h, 1, 2).start()
        x_copy(h, 1, 2, 1, 2).start()
        x_copy(h, 0, 1, 1, 1).wait_recv()
        d_copy(h, 1, 1).start()

    def take_last(h):
        x_copy(h, 0, 2, 0, 3).wait_recv()
        d_copy(h, 0, 3).start()
        x_copy(h, 1, 2, 1, 3).wait_recv()
        d_copy(h, 1, 3).start()

    def work(units):
        for e in range(2):
            pieces = [(h, 2 * pair + i) for _, h, pair, g in units if g == e for i in range(2)]
            pieces = [piece for piece in pieces if (piece, e) not in taken]
            taken.update((piece, e) for piece in pieces)

            @pl.when(jnp.logical_not(same) if e == 0 else same)
            def _(pieces=pieces):
                for h, d in pieces:
                    d_copy(h, 0, d, False).wait_recv()
                    d_copy(h, 1, d, False).wait_recv()

        tasks = [(h, pair, e, slice(*cols)) for columns, h, pair, e in units for cols in columns]
        state = {}

        def times(pair, e):
            return [2 * block(2 * pair + i) + (z if e == 0 else 1 - z) for i in range(2)]

        def scores(n):
            h, pair, e, cols = tasks[n]
            parts, tops = [], []
            for t in times(pair, e):
                s = lax.dot_general(kbuf[h, t], qbuf[h, cols], NT, preferred_element_type=jnp.float32)
                s = s.reshape(tok // 16, 16, -1)
                parts.append(s)
                tops.append(jnp.max(s, axis=0) + bias[t, :, cols])
            top = jnp.max(jnp.maximum(tops[0], tops[1]), axis=0, keepdims=True)
            before = peak[h, :1, cols]
            top = jnp.maximum(before, top)
            peak[h, :1, cols] = top
            state[n] = parts, top, jnp.exp2((before - top) * EXP_SCALE)

        def weigh(n):
            h, pair, e, cols = tasks[n]
            parts, top, fade = state[n]
            weights = []
            for t, s in zip(times(pair, e), parts):
                shift = (bias[t, :, cols] - top) * EXP_SCALE
                weights.append(jnp.exp2(s * EXP_SCALE + shift[None]).reshape(tok, -1).astype(jnp.bfloat16))
            state[n] = jnp.concatenate(weights, axis=0), fade

        def gather(n):
            h, pair, e, cols = tasks[n]
            weights, fade = state.pop(n)
            values = jnp.concatenate([vbuf[h, t] for t in times(pair, e)], axis=1)
            acc[h, :, cols] = acc[h, :, cols] * fade + jnp.dot(values, weights, preferred_element_type=jnp.float32)

        for n in range(len(tasks) + 2):
            if n < len(tasks):
                scores(n)
            if n >= 2:
                gather(n - 2)
            if 1 <= n <= len(tasks):
                weigh(n - 1)

    def chunks(h):
        if h < heads - 1:
            return ((h, 0, tok),)
        return tuple((h + i, lo, hi - lo) for i, (lo, hi) in enumerate(CHUNKS))

    def o_copies(h, act):
        for i, lo, width in chunks(h):

            def far(b, row, at, i=i, cols=pl.ds(lo, width)):
                return remote(
                    osend.at[h, b, :, cols], orecv.at[h, at, :, cols], o_s.at[i, b], o_r.at[i, at], dev(head, tm, row)
                )

            act(far(0, q_rows[1], jnp.where(y > 0, 1, 0)))
            pl.when(inner)(lambda far=far: act(far(1, y + 1, 0)))

    def log_of(h, cols):
        total = jnp.maximum(acc[h, HEAD_DIM : HEAD_DIM + 1, cols], 1e-30)
        return total, peak[h, :1, cols] * EXP_SCALE + jnp.log2(total)

    def finish(h):
        row = lax.broadcasted_iota(jnp.int32, (16, tok), 0)
        for b in (1, 2):
            cols = slice(b * tok, (b + 1) * tok)
            total, log = log_of(h, cols)
            osend[h, b - 1, :HEAD_DIM] = (acc[h, :HEAD_DIM, cols] * (1.0 / total)).astype(jnp.bfloat16)
            hi = log.astype(jnp.bfloat16).astype(jnp.float32)
            mid = (log - hi).astype(jnp.bfloat16).astype(jnp.float32)
            low = log - hi - mid
            osend[h, b - 1, HEAD_DIM:] = jnp.where(row == 0, hi, jnp.where(row == 1, mid, low)).astype(jnp.bfloat16)
        pl.when(jnp.logical_not(same))(lambda: o_copies(h, lambda copy: copy.start()))

    def finish_same(h):
        pl.when(same)(lambda: o_copies(h, lambda copy: copy.start()))

    def out_copy(h, part, local):
        i, lo, width = chunks(h)[part]
        src = done.at[h, pl.ds(lo, width)]
        dst = out_ref.at[pl.ds(lo, width), h * HEAD_DIM : (h + 1) * HEAD_DIM]
        if local:
            return pltpu.make_async_copy(src, dst, f_r.at[i])
        return remote(src, dst, f_s.at[i], f_r.at[i], partner)

    def merge(h, part=0):
        i, lo, width = chunks(h)[part]
        cols = slice(lo, lo + width)

        def far(at, row):
            ref = orecv.at[h, at, :, pl.ds(lo, width)]
            remote(ref, ref, o_s.at[i, 0], o_r.at[i, at], dev(head, tm, row)).wait_recv()

        pl.when(y > 0)(lambda: far(0, y - 1))
        pl.when(y < ny - 1)(lambda: far(1, y + 1))
        there = (y > 0, y < ny - 1)
        total, log = log_of(h, cols)
        logs, parts = [log], [acc[h, :HEAD_DIM, cols]]
        for at in range(2):
            tail = orecv[h, at, HEAD_DIM:, cols].astype(jnp.float32)
            logs.append(jnp.where(there[at], tail[0:1] + tail[1:2] + tail[2:3], -3e38))
            parts.append(jnp.where(there[at], orecv[h, at, :HEAD_DIM, cols].astype(jnp.float32), 0.0))
        top = jnp.maximum(jnp.maximum(logs[0], logs[1]), logs[2])
        shares = [jnp.exp2(log - top) for log in logs]
        scale = 1.0 / (shares[0] + shares[1] + shares[2])
        shares[0] = shares[0] / total
        result = sum(part * (share * scale) for part, share in zip(parts, shares))
        done[h, cols] = result.T.astype(jnp.bfloat16)
        pl.when(same)(lambda: out_copy(h, part, True).start())
        pl.when(jnp.logical_not(same))(lambda: out_copy(h, part, False).start())

    for h, i in [(h, i) for h in range(2) for i in range(3)] + [(2, 1), (2, 2), (2, 0)]:
        begin(h, i)
    prepare()
    for i in range(3):
        own_part(0, i)

    taken = set()
    steps = [
        ([(pass_on, 0)], [], [(OWN, 0, 0, 0)], []),
        (
            [(own_part, 2, 0), (own_part, 2, 1), (own_part, 2, 2), (pass_on, 1)]
            + [(own_part, 1, i) for i in range(3)]
            + [(q_wait, 0)],
            [(own_part, 1, 0), (own_part, 1, 1), (q_wait, 0)],
            [(NEAR, 0, 0, 0), (OWN, 1, 0, 0)],
            [],
        ),
        ([(take_last, 0)], [(own_part, 1, 2), (own_part, 2, 1)], [(NEAR, 0, 1, 0)], []),
        (
            [(q_wait, 1)],
            [(pass_on, 0), (own_part, 2, 2), (own_part, 2, 0), (q_wait, 1)],
            [(NEAR, 0, 0, 1), (NEAR, 1, 0, 0)],
            [],
        ),
        ([(pass_on, 2), (take_last, 1)], [], [(OWN, 0, 1, 0), (OWN, 0, 0, 1)], []),
        ([(q_wait, 2)], [(pass_on, 1), (q_wait, 2)], [(NEAR, 2, 0, 0), (NEAR, 1, 0, 1)], []),
        ([(take_last, 2)], [(take_last, 0)], [(NEAR, 1, 1, 0), (NEAR, 0, 1, 1)], [(finish, 0), (finish_same, 0)]),
        ([], [(pass_on, 2), (take_last, 1)], [(NEAR, 1, 1, 1), (NEAR, 2, 1, 0)], [(finish, 1), (finish_same, 1)]),
        ([], [], [(OWN, 0, 1, 1), (OWN, 1, 1, 0), (NEAR, 2, 0, 1)], []),
        ([], [(take_last, 2)], [(NEAR, 2, 1, 1)], [(finish, 2)]),
        ([], [], [(OWN, 1, 0, 1), (OWN, 1, 1, 1)], [(finish_same, 2), (merge, 0)]),
        ([], [], [(OWN, 2, 0, 0), (OWN, 2, 1, 0)], [(merge, 1)]),
        ([], [], [(OWN, 2, 0, 1), (OWN, 2, 1, 1)], [(merge, 2, 0), (merge, 2, 1)]),
    ]

    def do(acts):
        for act, *which in acts:
            act(*which)

    for acts_same, acts_swapped, units, acts_then in steps:
        pl.when(same)(lambda: do(acts_same))
        pl.when(jnp.logical_not(same))(lambda: do(acts_swapped))
        work(units)
        do(acts_then)

    for h in range(heads):
        for part in range(len(chunks(h))):
            pl.when(same)(lambda h=h, part=part: out_copy(h, part, True).wait())

            @pl.when(jnp.logical_not(same))
            def _(h=h, part=part):
                out_copy(h, part, False).wait_send()
                out_copy(h, part, False).wait_recv()

    def drain(h, carry):
        @pl.when(jnp.logical_not(same))
        def _():
            for i, (src, dst) in enumerate(
                ((qbuf.at[h, pl.ds(0, tok)], 0), (kbuf.at[h, 0], 0), (vt.at[h], 0))
            ):
                remote(src, src, swap_s.at[h, i], swap_r.at[h, i], partner).wait_send()

        for direction in range(2):
            x_copy(h, direction, 0, 0, 0).wait_send()
            x_copy(h, direction, 1, 1, 0).wait_send()
        x_copy(h, 0, 2, 0, 1).wait_send()
        x_copy(h, 1, 2, 1, 2).wait_send()
        for d in range(4):
            d_copy(h, 0, d).wait_send()
            d_copy(h, 1, d).wait_send()
        q_copies(h, lambda copy: copy.wait_send())
        return carry

    lax.fori_loop(0, heads, drain, 0)
    for h in range(heads):
        o_copies(h, lambda copy: copy.wait_send())


def solution(mesh):
    times = mesh.shape["tm"]

    def shards(queries, key_tokens, value_tokens, tile_mask):
        frames, rows, cols, chans = queries.shape
        tok = frames * rows * cols
        heads = chans // HEAD_DIM
        bf16, f32 = jnp.bfloat16, jnp.float32
        dma = pltpu.SemaphoreType.DMA
        out = pl.pallas_call(
            functools.partial(kernel, heads, tok),
            out_shape=jax.ShapeDtypeStruct((tok, chans), bf16),
            in_specs=[pl.BlockSpec(memory_space=pl.ANY)] * 4,
            out_specs=pl.BlockSpec(memory_space=pl.ANY),
            scratch_shapes=[
                pltpu.VMEM((heads, 3 * tok, HEAD_DIM), bf16),
                pltpu.VMEM((heads, times, tok, HEAD_DIM), bf16),
                pltpu.VMEM((heads, times, HEAD_DIM + 16, tok), bf16),
                pltpu.VMEM((tok, chans), bf16),
                pltpu.VMEM(tile_mask.shape, jnp.int32),
                pltpu.VMEM((heads, HEAD_DIM, tok), bf16),
                pltpu.VMEM((times, 16, 3 * tok), f32),
                pltpu.VMEM((heads, 8, 3 * tok), f32),
                pltpu.VMEM((heads, HEAD_DIM + 16, 3 * tok), f32),
                pltpu.VMEM((heads, 2, HEAD_DIM + 16, tok), bf16),
                pltpu.VMEM((heads, 2, HEAD_DIM + 16, tok), bf16),
                pltpu.VMEM((heads, tok, HEAD_DIM), bf16),
                dma((2,)),
                dma((heads, 3)), dma((heads, 3)),
                dma((heads, 2, 3)), dma((heads, 2, 3)),
                dma((heads, 4, 2)), dma((heads, 4, 2)),
                dma((heads, 2)), dma((heads, 2)),
                dma((heads + 1, 2)), dma((heads + 1, 2)),
                dma((heads + 1,)), dma((heads + 1,)),
            ],
            compiler_params=pltpu.CompilerParams(
                collective_id=0, has_side_effects=True, vmem_limit_bytes=536 * 2**20 // 10
            ),
        )(
            queries.reshape(tok, chans),
            key_tokens.reshape(tok, chans),
            value_tokens.reshape(tok, chans),
            tile_mask,
        )
        return out.reshape(frames, rows, cols, chans)

    return jax.shard_map(
        shards,
        mesh=mesh,
        in_specs=(
            P("tm", "height", None, "head"),
            P("tm", "height", None, "head"),
            P("tm", "height", None, "head"),
            P(),
        ),
        out_specs=P("tm", "height", None, "head"),
        check_vma=False,
    )
```
